32 devices in a mesh: dp: 2 (over core), row: 4 (over y, x), col: 4 (over z).
Axes of the slice: x: 2, y: 2, z: 4, core: 2. Of those that a mesh axis runs over, the one named last changes fastest.
Arguments:
- tokens: bfloat16 [384, 8192], P(('dp', 'col'), 'row'), may hold values from -160 to 160
- norm_gain: float32 [8192], P('row'), may hold values from 0.3 to 3
- gate_weight: bfloat16 [8192, 14336], P('row', ('dp', 'col')), may hold values from -0.0625 to 0.0625
- up_weight: bfloat16 [8192, 14336], P('row', ('dp', 'col')), may hold values from -0.0625 to 0.0625
- down_weight: bfloat16 [14336, 8192], P(('dp', 'col'), 'row'), may hold values from -0.046875 to 0.046875
- gate_keep: int32 [64, 112], P('row', ('dp', 'col')), may hold values from 0 to 1, as said below
- up_keep: int32 [64, 112], P('row', ('dp', 'col')), may hold values from 0 to 1, as said below
- down_keep: int32 [112, 64], P(('dp', 'col'), 'row'), may hold values from 0 to 1, as said below
- cotangent: bfloat16 [384, 8192], P(('dp', 'col'), 'row'), may hold values from -80 to 80
Outputs:
- branch: bfloat16 [384, 8192], P(('dp', 'col'), 'row')
- grad_tokens: float32 [384, 8192], P(('dp', 'col'), 'row')
- grad_gain: float32 [8192], P('row')
- grad_gate: float32 [8192, 14336], P('row', ('dp', 'col'))
- grad_up: float32 [8192, 14336], P('row', ('dp', 'col'))
- grad_down: float32 [14336, 8192], P(('dp', 'col'), 'row')
The draws below stay inside these ranges and needn't reach their ends.
Inputs may be any that keep to these rules, and one draw needn't show every extreme that they name: `gate_keep`: 1 keeps a 128 x 128 block of the gate projection, 0 prunes it. `up_keep`: 1 keeps a 128 x 128 block of the up projection, 0 prunes it. `down_keep`: 1 keeps a 128 x 128 block of the down projection, 0 prunes it.
All inputs are finite; a program needn't handle non-finite values.
Results may differ from the reference program's by a relative error of at most 0.0065.
Values may be sent and summed in bfloat16 or wider, within the bound.
No kernel may reach another device: no remote copies, remote signals or barrier semaphores. Data moves between devices by JAX's collectives and lax.ppermute only.
A program may use at most 320 MiB of HBM per device.

```python
import math
import jax
import jax.numpy as jnp
from jax import lax

D = 8192
FF = 14336
BLOCK = 128
TOKENS = 384


def keep_levels(key, salt, rows, cols, along_rows):
    level_key = jax.random.fold_in(key, salt)
    roll_key = jax.random.fold_in(key, salt + 1)
    if along_rows:
        level = jax.random.randint(level_key, (rows, 1), 1, 8)
    else:
        level = jax.random.randint(level_key, (1, cols), 1, 8)
    roll = jax.random.randint(roll_key, (rows, cols), 0, 8)
    return (roll < level).astype(jnp.int32)


def draw_gate_keep(key, part):
    return keep_levels(key, 101, D // BLOCK, FF // BLOCK, True)


def draw_up_keep(key, part):
    return keep_levels(key, 203, D // BLOCK, FF // BLOCK, True)


def draw_down_keep(key, part):
    return keep_levels(key, 307, FF // BLOCK, D // BLOCK, False)


def scaled_field(key, salt, col_ramp, row_ramp, col_hi, row_lo, row_hi):
    keys = [jax.random.fold_in(key, salt + step) for step in range(4)]
    col_factor = jnp.exp(jax.random.uniform(keys[0], (1, D), jnp.float32, 0.0, math.log(col_hi)))
    row_factor = jnp.exp(jax.random.uniform(keys[1], (TOKENS, 1), jnp.float32, math.log(row_lo), math.log(row_hi)))
    base = jnp.clip(jax.random.normal(keys[2], (TOKENS, D), jnp.float32), -4.0, 4.0)
    return base * col_factor * row_factor * col_ramp * row_ramp


def draw_tokens(key, part):
    col_ramp = 3.0 ** (jnp.arange(D, dtype=jnp.float32)[None, :] / D)
    row_ramp = jnp.ones((TOKENS, 1), jnp.float32)
    return scaled_field(key, 401, col_ramp, row_ramp, 3.3, 0.4, 4.0).astype(jnp.bfloat16)


def draw_cotangent(key, part):
    col_ramp = jnp.ones((1, D), jnp.float32)
    row_ramp = 3.0 ** (jnp.arange(TOKENS, dtype=jnp.float32)[:, None] / TOKENS)
    return scaled_field(key, 503, col_ramp, row_ramp, 2.0, 1.0, 3.3).astype(jnp.bfloat16)


def block_levels(rng, shape, cuts, low, high):
    level, own = 1.0, jax.random.fold_in(rng, 6)
    for axis_at, shards_of in cuts:
        draws = jnp.exp(jax.random.uniform(jax.random.fold_in(own, axis_at), (shards_of,), jnp.float32, low / len(cuts), high / len(cuts)))
        level = level * jnp.repeat(draws, shape[axis_at] // shards_of).reshape([-1 if axis == axis_at else 1 for axis in range(len(shape))])
    return level


def centred(key, extent, deviation, reach, cuts=(), held_as=jnp.bfloat16):
    loudness = block_levels(key, extent, cuts, -0.22, 0.18) if cuts else 1.0
    result = jax.random.normal(key, extent, jnp.float32) * deviation * loudness
    return jnp.minimum(jnp.maximum(result, -reach), reach).astype(held_as)


def setup_inputs(seed: int = 0) -> dict:
    arg_keys = jax.random.split(jax.random.key(seed), 10)
    return {
        "tokens": draw_tokens(jax.random.fold_in(arg_keys[9], 71), 0),
        "norm_gain": jnp.clip(jnp.exp(math.log(3.0) - 2.3025851 * jax.random.uniform(arg_keys[1], (D,), jnp.float32) ** block_levels(arg_keys[1], (D,), ((0, 4),), -0.2, 0.2)), 0.3, 3.0),
        "gate_weight": centred(arg_keys[2], (D, FF), D ** -0.5, 0.0625, ((0, 4), (1, 8))),
        "up_weight": centred(arg_keys[3], (D, FF), D ** -0.5, 0.0625, ((0, 4), (1, 8))),
        "down_weight": centred(arg_keys[4], (FF, D), FF ** -0.5, 0.046875, ((0, 8), (1, 4))),
        "gate_keep": draw_gate_keep(jax.random.fold_in(arg_keys[9], 71), 0),
        "up_keep": draw_up_keep(jax.random.fold_in(arg_keys[9], 71), 0),
        "down_keep": draw_down_keep(jax.random.fold_in(arg_keys[9], 71), 0),
        "cotangent": draw_cotangent(jax.random.fold_in(arg_keys[9], 71), 0),
    }


def expand_keep(keep, target_type):
    return jnp.repeat(jnp.repeat(keep, BLOCK, axis=0), BLOCK, axis=1).astype(target_type)

def reference(tokens, norm_gain, gate_weight, up_weight, down_weight, gate_keep, up_keep, down_keep, cotangent):
    token_f = tokens.astype(jnp.float32)
    inv_rms = lax.rsqrt(lax.optimization_barrier(jnp.mean(token_f * token_f, axis=1, keepdims=True)) + 1e-05)
    normed = (token_f * inv_rms * norm_gain).astype(jnp.bfloat16)
    gate_masked = gate_weight * expand_keep(gate_keep, jnp.bfloat16)
    up_masked = up_weight * expand_keep(up_keep, jnp.bfloat16)
    down_masked = down_weight * expand_keep(down_keep, jnp.bfloat16)
    gate = jnp.dot(normed, gate_masked, preferred_element_type=jnp.float32)
    up_value = jnp.dot(normed, up_masked, preferred_element_type=jnp.float32)
    sigmoid_gate = jax.nn.sigmoid(gate)
    hidden = (gate * sigmoid_gate * up_value).astype(jnp.bfloat16)
    branch = jnp.dot(hidden, down_masked, preferred_element_type=jnp.float32).astype(jnp.bfloat16)
    hidden_grad = jnp.dot(cotangent, down_masked.T, preferred_element_type=jnp.float32)
    gate_grad = (hidden_grad * up_value * sigmoid_gate * (1.0 + gate * (1.0 - sigmoid_gate))).astype(jnp.bfloat16)
    up_grad = (hidden_grad * gate * sigmoid_gate).astype(jnp.bfloat16)
    grad_down = jnp.dot(hidden.T, cotangent, preferred_element_type=jnp.float32) * expand_keep(down_keep, jnp.float32)
    grad_gate = jnp.dot(normed.T, gate_grad, preferred_element_type=jnp.float32) * expand_keep(gate_keep, jnp.float32)
    grad_up = jnp.dot(normed.T, up_grad, preferred_element_type=jnp.float32) * expand_keep(up_keep, jnp.float32)
    normed_grad = jnp.dot(gate_grad, gate_masked.T, preferred_element_type=jnp.float32) + jnp.dot(up_grad, up_masked.T, preferred_element_type=jnp.float32)
    grad_gain = lax.optimization_barrier(jnp.sum(normed_grad * token_f * inv_rms, axis=0))
    inner_dot = lax.optimization_barrier(jnp.sum(norm_gain * normed_grad * token_f, axis=1, keepdims=True))
    grad_tokens = inv_rms * norm_gain * normed_grad - token_f * inv_rms * inv_rms * inv_rms * inner_dot / D
    return (branch, grad_tokens, grad_gain, grad_gate, grad_up, grad_down)
```

```python
import functools
import jax
import jax.numpy as jnp
from jax import lax
from jax.experimental import pallas as pl
from jax.experimental.pallas import tpu as pltpu
from jax.sharding import PartitionSpec as P

BLOCK = 128
VMEM_BYTES = 44 * 1024 * 1024
BF16 = jnp.bfloat16
F32 = jnp.float32


def block_edge(extent):
    return 256 if extent % 256 == 0 else 128


def masked(weight, mask):
    groups, width = mask.shape
    shaped = weight.reshape(groups, BLOCK, width) * mask[:, None, :]
    return shaped.reshape(groups * BLOCK, width)


def swap(value, axis, size, step):
    return lax.ppermute(value, axis, [(i, i ^ step) for i in range(size)])


def shift(value, axis, size, step):
    return lax.ppermute(value, axis, [(i, (i + step) % size) for i in range(size)])


def kernel_params(steps):
    return pltpu.CompilerParams(
        dimension_semantics=("arbitrary",) * steps, vmem_limit_bytes=VMEM_BYTES
    )


def whole(shape):
    return pl.BlockSpec(shape, lambda *_: (0,) * len(shape))


def place_rows(result, plan, outs, lead):
    for ref, pieces in zip(outs, plan):
        at = 0
        for start, count in pieces:
            rows = result[start : start + count].astype(ref.dtype)
            if lead is None:
                ref[at : at + count, :] = rows
            else:
                ref[lead, at : at + count, :] = rows
            at += count


def plan_rows(pieces):
    return sum(count for _, count in pieces)


def project_kernel(ring, plan, by_unit, amount, place_ref, *refs):
    parts, refs = refs[: max(1, 2 * ring)], refs[max(1, 2 * ring) :]
    weights, masks, rows_ref, outs = refs[:amount], refs[amount : 2 * amount], refs[2 * amount], refs[2 * amount + 1 :]

    @pl.when(pl.program_id(0) == 0)
    def _():
        if not ring:
            rows_ref[...] = parts[0][...]
        else:
            place = place_ref[0]
            unit = parts[0].shape[0]
            for slot in range(ring):
                for source in range(ring):

                    @pl.when((place ^ slot) == source)
                    def _(slot=slot, source=source):
                        at = 2 * unit * slot
                        rows_ref[at : at + unit, :] = parts[source][...]
                        rows_ref[at + unit : at + 2 * unit, :] = parts[ring + source][...]

    rows = rows_ref[...]
    for lead, (weight, mask) in enumerate(zip(weights, masks)):
        if by_unit:
            result = lax.dot_general(
                rows, masked(weight[...], mask[0]), (((1,), (1,)), ((), ())), preferred_element_type=F32
            )
        else:
            result = jnp.dot(rows, masked(weight[...], mask[...]), preferred_element_type=F32)
        place_rows(result, plan, outs, lead)


def project(place, parts, weights, masks, plan, by_unit):
    ring = len(parts) // 2
    amount = len(weights)
    features = parts[0].shape[1]
    tokens = sum(part.shape[0] for part in parts)
    units = weights[0].shape[0] if by_unit else weights[0].shape[1]
    edge = block_edge(units)
    groups = features // BLOCK
    if by_unit:
        weight_spec = pl.BlockSpec((edge, features), lambda j, _: (j, 0))
        mask_spec = pl.BlockSpec((1, edge // BLOCK, features), lambda j, _: (j, 0, 0))
        masks = [mask.reshape(units // edge, edge // BLOCK, features) for mask in masks]
    else:
        weight_spec = pl.BlockSpec((features, edge), lambda j, _: (0, j))
        mask_spec = pl.BlockSpec((groups, edge), lambda j, _: (0, j))
    counts = [plan_rows(pieces) for pieces in plan]
    return pl.pallas_call(
        functools.partial(project_kernel, ring, plan, by_unit, amount),
        grid_spec=pltpu.PrefetchScalarGridSpec(
            num_scalar_prefetch=1,
            grid=(units // edge,),
            in_specs=[whole(part.shape) for part in parts] + [weight_spec] * amount + [mask_spec] * amount,
            out_specs=[whole((tokens, features))]
            + [pl.BlockSpec((amount, count, edge), lambda j, _: (0, 0, j)) for count in counts],
        ),
        out_shape=[jax.ShapeDtypeStruct((tokens, features), BF16)]
        + [jax.ShapeDtypeStruct((amount, count, units), BF16) for count in counts],
        compiler_params=kernel_params(1),
        cost_estimate=pl.CostEstimate(
            flops=2 * tokens * features * units * amount,
            bytes_accessed=2 * amount * features * units + 4 * tokens * features,
            transcendentals=0,
        ),
    )(place, *parts, *weights, *masks)


def contract_kernel(pieces, plan, by_unit, amount, *refs):
    parts, refs = refs[: len(pieces)], refs[len(pieces) :]
    weights, masks, rows_ref, outs = refs[:amount], refs[amount : 2 * amount], refs[2 * amount], refs[2 * amount + 1 :]

    @pl.when(pl.program_id(0) == 0)
    def _():
        at = 0
        for part, count in zip(parts, pieces):
            rows_ref[:, at : at + count, :] = part[...]
            at += count

    total = None
    for lead, (weight, mask) in enumerate(zip(weights, masks)):
        if by_unit:
            result = jnp.dot(rows_ref[lead], masked(weight[...], mask[...]), preferred_element_type=F32)
        else:
            result = lax.dot_general(
                rows_ref[lead],
                masked(weight[...], mask[0]),
                (((1,), (1,)), ((), ())),
                preferred_element_type=F32,
            )
        total = result if total is None else total + result
    place_rows(total, plan, outs, None)


def contract(parts, weights, masks, plan, types, by_unit):
    amount = len(weights)
    units = parts[0].shape[2]
    pieces = [part.shape[1] for part in parts]
    tokens = sum(pieces)
    features = weights[0].shape[1] if by_unit else weights[0].shape[0]
    edge = block_edge(features)
    if by_unit:
        weight_spec = pl.BlockSpec((units, edge), lambda j: (0, j))
        mask_spec = pl.BlockSpec((units // BLOCK, edge), lambda j: (0, j))
    else:
        weight_spec = pl.BlockSpec((edge, units), lambda j: (j, 0))
        mask_spec = pl.BlockSpec((1, edge // BLOCK, units), lambda j: (j, 0, 0))
        masks = [mask.reshape(features // edge, edge // BLOCK, units) for mask in masks]
    counts = [plan_rows(piece) for piece in plan]
    return pl.pallas_call(
        functools.partial(contract_kernel, pieces, plan, by_unit, amount),
        grid=(features // edge,),
        in_specs=[whole(part.shape) for part in parts] + [weight_spec] * amount + [mask_spec] * amount,
        out_specs=[whole((amount, tokens, units))]
        + [pl.BlockSpec((count, edge), lambda j: (0, j)) for count in counts],
        out_shape=[jax.ShapeDtypeStruct((amount, tokens, units), BF16)]
        + [jax.ShapeDtypeStruct((count, features), kind) for count, kind in zip(counts, types)],
        compiler_params=kernel_params(1),
        cost_estimate=pl.CostEstimate(
            flops=2 * tokens * features * units * amount,
            bytes_accessed=2 * amount * features * units + 4 * amount * tokens * units,
            transcendentals=0,
        ),
    )(*parts, *weights, *masks)


def outer_kernel(left_ref, right_ref, *refs):
    amount = right_ref.shape[0]
    masks, outs = refs[:amount], refs[amount:]
    for lead in range(amount):
        result = lax.dot_general(
            left_ref[...], right_ref[lead], (((0,), (0,)), ((), ())), preferred_element_type=F32
        )
        outs[lead][...] = masked(result, masks[lead][0].astype(F32))


def outer(left, right, masks):
    tokens, rows = left.shape
    amount, _, width = right.shape
    edge = block_edge(rows)
    masks = [mask.reshape(rows // edge, edge // BLOCK, width) for mask in masks]
    return pl.pallas_call(
        outer_kernel,
        grid=(rows // edge,),
        in_specs=[pl.BlockSpec((tokens, edge), lambda j: (0, j)), whole(right.shape)]
        + [pl.BlockSpec((1, edge // BLOCK, width), lambda j: (j, 0, 0))] * amount,
        out_specs=[pl.BlockSpec((edge, width), lambda j: (j, 0))] * amount,
        out_shape=[jax.ShapeDtypeStruct((rows, width), F32)] * amount,
        compiler_params=kernel_params(1),
        cost_estimate=pl.CostEstimate(
            flops=2 * tokens * rows * width * amount,
            bytes_accessed=4 * amount * rows * width + 2 * tokens * (rows + amount * width),
            transcendentals=0,
        ),
    )(left, right, *masks)


def activation(gate, up_value, hidden_grad):
    sigmoid_gate = 1.0 / (1.0 + jnp.exp(-gate))
    scaled = gate * sigmoid_gate
    hidden = scaled * up_value
    gate_grad = hidden_grad * up_value * sigmoid_gate * (1.0 + gate * (1.0 - sigmoid_gate))
    up_grad = hidden_grad * scaled
    return hidden, gate_grad, up_grad


def activate_kernel(pair0, pair_x, pair_y, pair_y2, pair_x2, one0, one_x, one_y, one_y2, one_x2, hidden_ref, grads_ref):
    half = pair_y2.shape[1]

    def summed(refs, lead, second):
        own, first_x, first_y, last_y, last_x = refs
        first, last = (first_y, last_x) if second else (first_x, last_y)
        at = half if second else 0
        return (
            own[lead, at : at + half, :].astype(F32)
            + first[lead, half:, :].astype(F32)
            + last[lead].astype(F32)
        )

    pair = (pair0, pair_x, pair_y, pair_y2, pair_x2)
    one = (one0, one_x, one_y, one_y2, one_x2)
    for second in (False, True):
        at = half if second else 0
        results = activation(summed(pair, 0, second), summed(pair, 1, second), summed(one, 0, second))
        hidden_ref[0, at : at + half, :] = results[0].astype(BF16)
        grads_ref[0, at : at + half, :] = results[1].astype(BF16)
        grads_ref[1, at : at + half, :] = results[2].astype(BF16)


def activate(pair, one):
    _, share, units = pair[0].shape
    edge = block_edge(units)
    spec = lambda array: pl.BlockSpec(array.shape[:2] + (edge,), lambda j: (0, 0, j))
    outs = [jax.ShapeDtypeStruct((amount, share, units), BF16) for amount in (1, 2)]
    return pl.pallas_call(
        activate_kernel,
        grid=(units // edge,),
        in_specs=[spec(array) for array in pair + one],
        out_specs=[spec(array) for array in outs],
        out_shape=outs,
        compiler_params=kernel_params(1),
    )(*pair, *one)


def widen(keep):
    return jnp.repeat(keep, BLOCK, axis=1).astype(BF16)


def finish(token_f, inv_rms, norm_gain, normed_grad, inner_sum, gain_sum):
    grad_gain = gain_sum(jnp.sum(normed_grad * token_f * inv_rms, axis=0))
    inner_dot = inner_sum(jnp.sum(norm_gain * normed_grad * token_f, axis=1))
    width = norm_gain.shape[0] * lax.axis_size("row")
    grad_tokens = (
        inv_rms * norm_gain * normed_grad
        - token_f * inv_rms * inv_rms * inv_rms * inner_dot[:, None] / width
    )
    return grad_tokens, grad_gain


def exchange_device(
    tokens, norm_gain, gate_weight, up_weight, down_weight, gate_keep, up_keep, down_keep, cotangent
):
    rows, cols = 4, 4
    unit, features = tokens.shape
    place = lax.axis_index("row")
    place_arg = place.astype(jnp.int32).reshape(1)
    level = lax.axis_index("col")

    def row_sum(value):
        return value + swap(value, "row", rows, 1) + swap(value, "row", rows, 2) + swap(value, "row", rows, 3)

    def spread(value):
        own = [value] + [shift(value, "col", cols, step) for step in range(1, cols)]
        return own + [swap(part, "dp", 2, 1) for part in own]

    def exchange_sum(x_first, y_first, x_keep, y_keep, kept):
        half = x_keep.shape[1]
        got_x = swap(x_first, "row", rows, 1)
        got_y = swap(y_first, "row", rows, 2)
        add = lambda a, b: (a.astype(F32) + b[:, :half].astype(F32)).astype(BF16)
        last_y = swap(add(y_keep, got_x), "row", rows, 2)
        last_x = swap(add(x_keep, got_y), "row", rows, 1)
        return [kept, got_x, got_y, last_y, last_x]

    def exchange_gather(share):
        half = share.shape[1] // 2
        got_x = swap(share, "row", rows, 1)
        got_y = swap(share, "row", rows, 2)
        far_x = swap(got_y[:, :half], "row", rows, 1)
        far_y = swap(got_x[:, half:], "row", rows, 2)
        return [share, got_x, got_y, far_x, far_y]

    def owner_sum(own, other):
        got = swap(other, "dp", 2, 1)
        total = None
        for step in range(cols):
            at = (place ^ step) * unit
            part = lax.dynamic_slice_in_dim(own, at, unit, 0) + lax.dynamic_slice_in_dim(got, at, unit, 0).astype(F32)
            if step:
                part = shift(part.astype(BF16), "col", cols, -step).astype(F32)
            total = part if total is None else total + part
        return total

    def gain_sum(value):
        value = value + swap(value, "dp", 2, 1)
        parts = jnp.stack([value] + [shift(value, "col", cols, step) for step in range(1, cols)])
        return jnp.sum(jnp.take(parts, (level - jnp.arange(cols)) % cols, axis=0), axis=0)

    token_f = tokens.astype(F32)
    square = row_sum(jnp.sum(token_f * token_f, axis=1))
    inv_rms = lax.rsqrt(square[:, None] / (features * rows) + 1e-05)
    normed = (token_f * inv_rms * norm_gain).astype(BF16)
    gate_mask, up_mask, down_mask = widen(gate_keep), widen(up_keep), widen(down_keep)

    def rows_of(slot, second):
        return (2 * unit * slot + (unit if second else 0), unit)

    first_plan = [
        [rows_of(3, False), rows_of(1, False)],
        [rows_of(3, True), rows_of(2, True)],
        [rows_of(1, True)],
        [rows_of(2, False)],
        [(0, 2 * unit)],
    ]
    last_plan = [[rows_of(slot, False) for slot in range(rows)], [rows_of(slot, True) for slot in range(rows)]]

    seen_cot, *grad_parts = project(place_arg, spread(cotangent), [down_weight], [down_mask], first_plan, True)
    one = exchange_sum(*grad_parts)
    seen_rows, *pair_parts = project(
        place_arg, spread(normed), [gate_weight, up_weight], [gate_mask, up_mask], first_plan, False
    )
    pair = exchange_sum(*pair_parts)
    hidden_share, grads_share = activate(pair, one)
    hidden, branch_own, branch_other = contract(
        exchange_gather(hidden_share), [down_weight], [down_mask], last_plan, (F32, BF16), True
    )
    branch = owner_sum(branch_own, branch_other).astype(BF16)
    (grad_down,) = outer(hidden[0], seen_cot[None], [down_mask])
    grads, normed_own, normed_other = contract(
        exchange_gather(grads_share), [gate_weight, up_weight], [gate_mask, up_mask], last_plan, (F32, BF16), False
    )
    normed_grad = owner_sum(normed_own, normed_other)
    grad_gate, grad_up = outer(seen_rows, grads, [gate_mask, up_mask])
    grad_tokens, grad_gain = finish(token_f, inv_rms, norm_gain, normed_grad, row_sum, gain_sum)
    return (branch, grad_tokens, grad_gain, grad_gate, grad_up, grad_down)


def general_device(
    tokens, norm_gain, gate_weight, up_weight, down_weight, gate_keep, up_keep, down_keep, cotangent
):
    owners = ("dp", "col")
    features = tokens.shape[1]
    place_arg = jnp.zeros((1,), jnp.int32)
    token_f = tokens.astype(F32)
    square = lax.psum(jnp.sum(token_f * token_f, axis=1), "row")
    inv_rms = lax.rsqrt(square[:, None] / (features * lax.axis_size("row")) + 1e-05)
    normed = (token_f * inv_rms * norm_gain).astype(BF16)
    gate_mask, up_mask, down_mask = widen(gate_keep), widen(up_keep), widen(down_keep)
    seen_cot = lax.all_gather(cotangent, owners, axis=0, tiled=True)
    seen_rows = lax.all_gather(normed, owners, axis=0, tiled=True)
    plan = [[(0, seen_cot.shape[0])]]

    def share(value):
        return lax.psum_scatter(value.astype(F32), "row", scatter_dimension=1, tiled=True)

    def collect(value):
        return lax.all_gather(value.astype(BF16), "row", axis=1, tiled=True)

    def owner_sum(value):
        return lax.psum_scatter(value, owners, scatter_dimension=0, tiled=True)

    _, one = project(place_arg, [seen_cot], [down_weight], [down_mask], plan, True)
    _, pair = project(place_arg, [seen_rows], [gate_weight, up_weight], [gate_mask, up_mask], plan, False)
    pair = share(pair)
    hidden, gate_grad, up_grad = activation(pair[0], pair[1], share(one)[0])
    hidden, branch = contract([collect(hidden[None])], [down_weight], [down_mask], plan, (F32,), True)
    branch = owner_sum(branch).astype(BF16)
    grads, normed_grad = contract(
        [collect(jnp.stack([gate_grad, up_grad]))], [gate_weight, up_weight], [gate_mask, up_mask], plan, (F32,), False
    )
    normed_grad = owner_sum(normed_grad)
    (grad_down,) = outer(hidden[0], seen_cot[None], [down_mask])
    grad_gate, grad_up = outer(seen_rows, grads, [gate_mask, up_mask])
    grad_tokens, grad_gain = finish(
        token_f,
        inv_rms,
        norm_gain,
        normed_grad,
        lambda value: lax.psum(value, "row"),
        lambda value: lax.psum(value, owners),
    )
    return (branch, grad_tokens, grad_gain, grad_gate, grad_up, grad_down)


def solution(mesh):
    split = P(("dp", "col"), "row")
    turned = P("row", ("dp", "col"))
    sizes = (mesh.shape["dp"], mesh.shape["row"], mesh.shape["col"])
    on_device = exchange_device if sizes == (2, 4, 4) else general_device
    return jax.shard_map(
        on_device,
        mesh=mesh,
        in_specs=(split, P("row"), turned, turned, split, turned, turned, split, split),
        out_specs=(split, split, P("row"), turned, turned, split),
        check_vma=False,
    )
```

```python
import functools
import jax
import jax.numpy as jnp
from jax import lax
from jax.experimental import pallas as pl
from jax.experimental.pallas import tpu as pltpu
from jax.sharding import PartitionSpec as P

BLOCK = 128
VMEM_BYTES = 10 * 1024 * 1024
BF16 = jnp.bfloat16
F32 = jnp.float32


def block_edge(extent):
    return 256 if extent % 256 == 0 else 128


def masked(weight, mask):
    groups, width = mask.shape
    shaped = weight.reshape(groups, BLOCK, width) * mask[:, None, :]
    return shaped.reshape(groups * BLOCK, width)


def swap(value, axis, size, step):
    return lax.ppermute(value, axis, [(i, i ^ step) for i in range(size)])


def kernel_params(steps=0):
    return pltpu.CompilerParams(
        dimension_semantics=("arbitrary",) * steps if steps else None, vmem_limit_bytes=VMEM_BYTES
    )


IN_VMEM = pl.BlockSpec(memory_space=pltpu.VMEM)
IN_SMEM = pl.BlockSpec(memory_space=pltpu.SMEM)


def place_rows(result, plan, outs, lead, columns):
    for ref, pieces in zip(outs, plan):
        at = 0
        for start, count in pieces:
            rows = result[start : start + count].astype(ref.dtype)
            if lead is None:
                ref[at : at + count, columns] = rows
            else:
                ref[lead, at : at + count, columns] = rows
            at += count


def plan_rows(pieces):
    return sum(count for _, count in pieces)


def project_kernel(ring, plan, by_unit, amount, place_ref, *refs):
    parts, refs = refs[: max(1, 2 * ring)], refs[max(1, 2 * ring) :]
    weights, masks, rows_ref, outs = refs[:amount], refs[amount : 2 * amount], refs[2 * amount], refs[2 * amount + 1 :]
    if not ring:
        rows_ref[...] = parts[0][...]
    else:
        place = place_ref[0]
        unit = parts[0].shape[0]
        for slot in range(ring):
            for source in range(ring):

                @pl.when((place ^ slot) == source)
                def _(slot=slot, source=source):
                    at = 2 * unit * slot
                    rows_ref[at : at + unit, :] = parts[source][...]
                    rows_ref[at + unit : at + 2 * unit, :] = parts[ring + source][...]

    rows = rows_ref[...]
    units = weights[0].shape[0] if by_unit else weights[0].shape[1]
    edge = block_edge(units)
    for lead, (weight, mask) in enumerate(zip(weights, masks)):
        for at in range(0, units, edge):
            columns = slice(at, at + edge)
            if by_unit:
                kept = masked(weight[columns, :], mask[at // BLOCK : (at + edge) // BLOCK, :])
                result = lax.dot_general(rows, kept, (((1,), (1,)), ((), ())), preferred_element_type=F32)
            else:
                kept = masked(weight[:, columns], mask[:, columns])
                result = jnp.dot(rows, kept, preferred_element_type=F32)
            place_rows(result, plan, outs, lead, columns)


def project(place, parts, weights, masks, plan, by_unit):
    ring = len(parts) // 2
    amount = len(weights)
    features = parts[0].shape[1]
    tokens = sum(part.shape[0] for part in parts)
    units = weights[0].shape[0] if by_unit else weights[0].shape[1]
    counts = [plan_rows(pieces) for pieces in plan]
    return pl.pallas_call(
        functools.partial(project_kernel, ring, plan, by_unit, amount),
        in_specs=[IN_SMEM] + [IN_VMEM] * (len(parts) + 2 * amount),
        out_specs=[IN_VMEM] * (1 + len(plan)),
        out_shape=[jax.ShapeDtypeStruct((tokens, features), BF16)]
        + [jax.ShapeDtypeStruct((amount, count, units), BF16) for count in counts],
        compiler_params=kernel_params(),
        cost_estimate=pl.CostEstimate(
            flops=2 * tokens * features * units * amount,
            bytes_accessed=2 * amount * features * units,
            transcendentals=0,
        ),
    )(place, *parts, *weights, *masks)


def contract_kernel(pieces, plan, by_unit, amount, *refs):
    parts, refs = refs[: len(pieces)], refs[len(pieces) :]
    weights, masks, rows_ref, outs = refs[:amount], refs[amount : 2 * amount], refs[2 * amount], refs[2 * amount + 1 :]
    at = 0
    for part, count in zip(parts, pieces):
        rows_ref[:, at : at + count, :] = part[...]
        at += count
    rows = [rows_ref[lead] for lead in range(amount)]
    features = weights[0].shape[1] if by_unit else weights[0].shape[0]
    edge = block_edge(features)
    for at in range(0, features, edge):
        columns = slice(at, at + edge)
        total = None
        for lead, (weight, mask) in enumerate(zip(weights, masks)):
            if by_unit:
                kept = masked(weight[:, columns], mask[:, columns])
                result = jnp.dot(rows[lead], kept, preferred_element_type=F32)
            else:
                kept = masked(weight[columns, :], mask[at // BLOCK : (at + edge) // BLOCK, :])
                result = lax.dot_general(rows[lead], kept, (((1,), (1,)), ((), ())), preferred_element_type=F32)
            total = result if total is None else total + result
        place_rows(total, plan, outs, None, columns)


def contract(parts, weights, masks, plan, types, by_unit):
    amount = len(weights)
    units = parts[0].shape[2]
    pieces = [part.shape[1] for part in parts]
    tokens = sum(pieces)
    features = weights[0].shape[1] if by_unit else weights[0].shape[0]
    counts = [plan_rows(piece) for piece in plan]
    return pl.pallas_call(
        functools.partial(contract_kernel, pieces, plan, by_unit, amount),
        in_specs=[IN_VMEM] * (len(parts) + 2 * amount),
        out_specs=[IN_VMEM] * (1 + len(plan)),
        out_shape=[jax.ShapeDtypeStruct((amount, tokens, units), BF16)]
        + [jax.ShapeDtypeStruct((count, features), kind) for count, kind in zip(counts, types)],
        compiler_params=kernel_params(),
        cost_estimate=pl.CostEstimate(
            flops=2 * tokens * features * units * amount,
            bytes_accessed=2 * amount * features * units,
            transcendentals=0,
        ),
    )(*parts, *weights, *masks)


def outer_kernel(left_ref, right_ref, *refs):
    amount = right_ref.shape[0]
    masks, outs = refs[:amount], refs[amount:]
    edge = outs[0].shape[0]
    left = left_ref[:, pl.ds(pl.multiple_of(pl.program_id(0) * edge, edge), edge)]
    for lead in range(amount):
        result = lax.dot_general(left, right_ref[lead], (((0,), (0,)), ((), ())), preferred_element_type=F32)
        outs[lead][...] = masked(result, masks[lead][0].astype(F32))


def outer(left, right, masks):
    tokens, rows = left.shape
    amount, _, width = right.shape
    edge = block_edge(rows)
    return pl.pallas_call(
        outer_kernel,
        grid=(rows // edge,),
        in_specs=[IN_VMEM, IN_VMEM] + [pl.BlockSpec((1, edge // BLOCK, width), lambda j: (j, 0, 0))] * amount,
        out_specs=[pl.BlockSpec((edge, width), lambda j: (j, 0))] * amount,
        out_shape=[jax.ShapeDtypeStruct((rows, width), F32)] * amount,
        compiler_params=kernel_params(1),
        cost_estimate=pl.CostEstimate(
            flops=2 * tokens * rows * width * amount,
            bytes_accessed=4 * amount * rows * width,
            transcendentals=0,
        ),
    )(left, right, *masks)


def owner_kernel(count, place_ref, own_ref, got_ref, *refs):
    factors, outs, sums = refs[:-count], refs[-count:], ()
    if factors:
        factors, outs, sums = refs[:count], refs[count : 2 * count], refs[2 * count :]
    unit = outs[0].shape[0]
    place = place_ref[0]
    down = None
    for step in range(count):
        rows = pl.ds(pl.multiple_of((place ^ step) * unit, 16), unit)
        part = own_ref[rows, :] + got_ref[rows, :].astype(F32)
        outs[step][...] = part.astype(outs[step].dtype)
        if factors:
            product = part * factors[step][...].astype(F32)
            across = jnp.sum(product, axis=1, keepdims=True)
            sums[0][step * unit : (step + 1) * unit, :] = jnp.broadcast_to(across, (unit, sums[0].shape[1]))
            step_down = jnp.sum(product, axis=0, keepdims=True)
            down = step_down if down is None else down + step_down
    if factors:
        sums[1][...] = down


def owner(place, own, got, count, factors=()):
    total, features = own.shape
    unit = total // count
    outs = [jax.ShapeDtypeStruct((unit, features), F32 if step == 0 else BF16) for step in range(count)]
    if factors:
        outs += [jax.ShapeDtypeStruct((total, 128), F32), jax.ShapeDtypeStruct((1, features), F32)]
    return pl.pallas_call(
        functools.partial(owner_kernel, count),
        in_specs=[IN_SMEM] + [IN_VMEM] * (2 + len(factors)),
        out_specs=[IN_VMEM] * len(outs),
        out_shape=outs,
        compiler_params=kernel_params(),
    )(place, own, got, *factors)


def activation(gate, up_value, hidden_grad):
    sigmoid_gate = 1.0 / (1.0 + jnp.exp(-gate))
    scaled = gate * sigmoid_gate
    hidden = scaled * up_value
    gate_grad = hidden_grad * up_value * sigmoid_gate * (1.0 + gate * (1.0 - sigmoid_gate))
    up_grad = hidden_grad * scaled
    return hidden, gate_grad, up_grad


def activate_kernel(*refs):
    pair, one, (hidden_ref, grads_ref) = refs[:5], refs[5:10], refs[10:]
    half = pair[3].shape[1]
    for second in (False, True):
        at = half if second else 0
        rows = slice(at, at + half)

        def summed(parts, lead):
            own, first_x, first_y, last_y, last_x = parts
            first, last = (first_y, last_x) if second else (first_x, last_y)
            return own[lead, rows].astype(F32) + first[lead, half:].astype(F32) + last[lead].astype(F32)

        results = activation(summed(pair, 0), summed(pair, 1), summed(one, 0))
        hidden_ref[0, rows] = results[0].astype(BF16)
        grads_ref[0, rows] = results[1].astype(BF16)
        grads_ref[1, rows] = results[2].astype(BF16)


def activate(pair, one):
    _, share, units = pair[0].shape
    edge = block_edge(units)
    spec = lambda array: pl.BlockSpec(array.shape[:2] + (edge,), lambda j: (0, 0, j))
    outs = [jax.ShapeDtypeStruct((amount, share, units), BF16) for amount in (1, 2)]
    return pl.pallas_call(
        activate_kernel,
        grid=(units // edge,),
        in_specs=[spec(array) for array in pair + one],
        out_specs=[spec(array) for array in outs],
        out_shape=outs,
        compiler_params=kernel_params(1),
    )(*pair, *one)


def widen(keep):
    return jnp.repeat(keep, BLOCK, axis=1).astype(BF16)


def widen_grouped(keep):
    together = block_edge(keep.shape[0] * BLOCK) // BLOCK
    return widen(keep).reshape(-1, together, keep.shape[1] * BLOCK)


def finish(token_f, inv_rms, norm_gain, normed_grad, inner_sum, gain_sum):
    grad_gain = gain_sum(jnp.sum(normed_grad * token_f * inv_rms, axis=0))
    inner_dot = inner_sum(jnp.sum(norm_gain * normed_grad * token_f, axis=1))
    width = norm_gain.shape[0] * lax.axis_size("row")
    grad_tokens = (
        inv_rms * norm_gain * normed_grad
        - token_f * inv_rms * inv_rms * inv_rms * inner_dot[:, None] / width
    )
    return grad_tokens, grad_gain


def ordered(*groups):
    return lax.optimization_barrier(groups)


def exchange_device(
    tokens, norm_gain, gate_weight, up_weight, down_weight, gate_keep, up_keep, down_keep, cotangent
):
    rows, cols = 4, 4
    unit, features = tokens.shape
    place = lax.axis_index("row")
    place_arg = place.astype(jnp.int32).reshape(1)

    def core_swap(value):
        return swap(value, "dp", 2, 1)

    def row_swap(value, step):
        return swap(value, "row", rows, step)

    def level_swaps(parts):
        return [swap(part, "col", cols, step + 1) for step, part in enumerate(parts)]

    def balanced(value, got):
        return (value + got[0]) + (got[1] + got[2])

    def row_sum(value):
        value = value + row_swap(value, 1)
        return value + row_swap(value, 2)

    def sum_first(x_first, y_first):
        return ordered(row_swap(x_first, 1), row_swap(y_first, 2))

    def sum_middle(x_keep, y_keep, got_x, got_y):
        half = x_keep.shape[1]
        add = lambda a, b: (a.astype(F32) + b[:, :half].astype(F32)).astype(BF16)
        return add(y_keep, got_x), add(x_keep, got_y)

    def sum_last(for_y, for_x):
        return ordered(row_swap(for_y, 2), row_swap(for_x, 1))

    def gather_first(share):
        return ordered(row_swap(share, 1), row_swap(share, 2))

    def gather_middle(got_x, got_y):
        return got_y[:, :unit], got_x[:, unit:]

    def gather_last(for_x, for_y):
        return ordered(row_swap(for_x, 1), row_swap(for_y, 2))

    def owner_total(kept, got):
        return balanced(kept, [part.astype(F32) for part in got])

    def rows_of(slot, second):
        return (2 * unit * slot + (unit if second else 0), unit)

    first_plan = [
        [rows_of(3, False), rows_of(1, False)],
        [rows_of(3, True), rows_of(2, True)],
        [rows_of(1, True)],
        [rows_of(2, False)],
        [(0, 2 * unit)],
    ]
    last_plan = [[rows_of(slot, False) for slot in range(rows)], [rows_of(slot, True) for slot in range(rows)]]

    token_f = tokens.astype(F32)
    squares = jnp.sum(token_f * token_f, axis=1)
    cot_far = level_swaps([cotangent] * 3)
    inv_rms = lax.rsqrt(row_sum(squares)[:, None] / (features * rows) + 1e-05)
    normed = (token_f * inv_rms * norm_gain).astype(BF16)
    gate_mask, up_mask, down_mask = widen(gate_keep), widen(up_keep), widen(down_keep)
    gate_groups, up_groups, down_groups = widen_grouped(gate_keep), widen_grouped(up_keep), widen_grouped(down_keep)
    normed_core = core_swap(normed)
    masks = [gate_mask, up_mask, down_mask, gate_groups, up_groups, down_groups]
    cot_far, normed, normed_core, place, place_arg, masks = ordered(
        cot_far, normed, normed_core, place, place_arg, masks
    )
    gate_mask, up_mask, down_mask, gate_groups, up_groups, down_groups = masks
    cot_own = [cotangent, *cot_far]
    cot_other = [core_swap(part) for part in cot_own]

    normed_far = level_swaps([normed] * 3)
    seen_cot, *one_parts = project(place_arg, cot_own + cot_other, [down_weight], [down_mask], first_plan, True)
    one_x, one_y = sum_first(*one_parts[:2])
    one_keep = one_parts[2:]
    normed_far, one_x, one_y = ordered(normed_far, one_x, one_y)
    normed_own = [normed, *normed_far]
    normed_other = [normed_core] + [core_swap(part) for part in normed_far]
    one_late = sum_middle(*one_keep[:2], one_x, one_y)
    normed_other, one_late = ordered(normed_other, one_late)

    one_last = sum_last(*one_late)
    seen_rows, *pair_parts = project(place_arg, normed_own + normed_other, [gate_weight, up_weight], [gate_mask, up_mask], first_plan, False)
    one_last, pair_parts = ordered(one_last, pair_parts)
    pair_x, pair_y = sum_first(*pair_parts[:2])
    pair_last = sum_last(*sum_middle(*pair_parts[2:4], pair_x, pair_y))
    hidden_share, grads_share = activate(
        [pair_parts[4], pair_x, pair_y, *pair_last], [one_keep[2], one_x, one_y, *one_last]
    )

    hidden_x, hidden_y = gather_first(hidden_share)
    hidden_middle = gather_middle(hidden_x, hidden_y)
    grads_share, hidden_middle = ordered(grads_share, hidden_middle)
    grads_x, grads_y = gather_first(grads_share)
    hidden_last = gather_last(*hidden_middle)
    hidden, branch_own, branch_other = contract(
        [hidden_share, hidden_x, hidden_y, *hidden_last], [down_weight], [down_mask], last_plan, (F32, BF16), True
    )
    grads_x, grads_y, branch_own, branch_other = ordered(grads_x, grads_y, branch_own, branch_other)
    branch_got = core_swap(branch_other)
    grads_middle = gather_middle(grads_x, grads_y)
    grads_last = gather_last(*grads_middle)
    branch_kept, *branch_parts = owner(place_arg, branch_own, branch_got, cols)
    hidden, branch_parts = ordered(hidden, branch_parts)
    branch_far = level_swaps(branch_parts)
    (grad_down,) = outer(hidden[0], seen_cot[None], [down_groups])
    grads_last, grad_down = ordered(grads_last, grad_down)

    grads, normed_mine, normed_theirs = contract(
        [grads_share, grads_x, grads_y, *grads_last], [gate_weight, up_weight], [gate_mask, up_mask], last_plan, (F32, BF16), False
    )
    branch_far, normed_mine, normed_theirs = ordered(branch_far, normed_mine, normed_theirs)
    kept, *parts, across, down_sum = owner(place_arg, normed_mine, core_swap(normed_theirs), cols, normed_own)
    grads, parts, across, down_sum = ordered(grads, parts, across, down_sum)
    far = level_swaps(parts)
    across_x = across + row_swap(across, 1)
    down_both = down_sum + core_swap(down_sum)
    across_x, down_both, grads = ordered(across_x, down_both, grads)
    across_row = across_x + row_swap(across_x, 2)
    grad_gate, grad_up = outer(seen_rows, grads, [gate_groups, up_groups])
    far, across_row, down_both, grad_gate, grad_up = ordered(far, across_row, down_both, grad_gate, grad_up)
    sums = [
        jnp.concatenate([across_row[step * unit : (step + 1) * unit], down_both.reshape(-1, 128)])
        for step in range(cols)
    ]
    sums_total = balanced(sums[0], level_swaps(sums[1:]))
    branch = owner_total(branch_kept, branch_far).astype(BF16)
    normed_grad = owner_total(kept, far)
    grad_gain = sums_total[unit:].reshape(features) / norm_gain
    grad_tokens = (
        inv_rms * norm_gain * normed_grad - token_f * inv_rms * inv_rms * sums_total[:unit, :1] / (features * rows)
    )
    return (branch, grad_tokens, grad_gain, grad_gate, grad_up, grad_down)


def general_device(
    tokens, norm_gain, gate_weight, up_weight, down_weight, gate_keep, up_keep, down_keep, cotangent
):
    owners = ("dp", "col")
    features = tokens.shape[1]
    place_arg = jnp.zeros((1,), jnp.int32)
    token_f = tokens.astype(F32)
    square = lax.psum(jnp.sum(token_f * token_f, axis=1), "row")
    inv_rms = lax.rsqrt(square[:, None] / (features * lax.axis_size("row")) + 1e-05)
    normed = (token_f * inv_rms * norm_gain).astype(BF16)
    gate_mask, up_mask, down_mask = widen(gate_keep), widen(up_keep), widen(down_keep)
    gate_groups, up_groups, down_groups = widen_grouped(gate_keep), widen_grouped(up_keep), widen_grouped(down_keep)
    seen_cot = lax.all_gather(cotangent, owners, axis=0, tiled=True)
    seen_rows = lax.all_gather(normed, owners, axis=0, tiled=True)
    plan = [[(0, seen_cot.shape[0])]]

    def share(value):
        return lax.psum_scatter(value.astype(F32), "row", scatter_dimension=1, tiled=True)

    def collect(value):
        return lax.all_gather(value.astype(BF16), "row", axis=1, tiled=True)

    def owner_sum(value):
        return lax.psum_scatter(value, owners, scatter_dimension=0, tiled=True)

    _, one = project(place_arg, [seen_cot], [down_weight], [down_mask], plan, True)
    _, pair = project(place_arg, [seen_rows], [gate_weight, up_weight], [gate_mask, up_mask], plan, False)
    pair = share(pair)
    hidden, gate_grad, up_grad = activation(pair[0], pair[1], share(one)[0])
    hidden, branch = contract([collect(hidden[None])], [down_weight], [down_mask], plan, (F32,), True)
    branch = owner_sum(branch).astype(BF16)
    grads, normed_grad = contract(
        [collect(jnp.stack([gate_grad, up_grad]))], [gate_weight, up_weight], [gate_mask, up_mask], plan, (F32,), False
    )
    normed_grad = owner_sum(normed_grad)
    (grad_down,) = outer(hidden[0], seen_cot[None], [down_groups])
    grad_gate, grad_up = outer(seen_rows, grads, [gate_groups, up_groups])
    grad_tokens, grad_gain = finish(
        token_f,
        inv_rms,
        norm_gain,
        normed_grad,
        lambda value: lax.psum(value, "row"),
        lambda value: lax.psum(value, owners),
    )
    return (branch, grad_tokens, grad_gain, grad_gate, grad_up, grad_down)


def solution(mesh):
    split = P(("dp", "col"), "row")
    turned = P("row", ("dp", "col"))
    sizes = (mesh.shape["dp"], mesh.shape["row"], mesh.shape["col"])
    on_device = exchange_device if sizes == (2, 4, 4) else general_device
    return jax.shard_map(
        on_device,
        mesh=mesh,
        in_specs=(split, P("row"), turned, turned, split, turned, turned, split, split),
        out_specs=(split, split, P("row"), turned, turned, split),
        check_vma=False,
    )
```

```python
import functools
import jax
import jax.numpy as jnp
from jax import lax
from jax.experimental import pallas as pl
from jax.experimental.pallas import tpu as pltpu
from jax.sharding import PartitionSpec as P

BLOCK = 128
VMEM_BYTES = 10 * 1024 * 1024
BF16 = jnp.bfloat16
F32 = jnp.float32


def block_edge(extent):
    return 256 if extent % 256 == 0 else 128


def masked(weight, mask):
    groups, width = mask.shape
    shaped = weight.reshape(groups, BLOCK, width) * mask[:, None, :]
    return shaped.reshape(groups * BLOCK, width)


def swap(value, axis, size, step):
    return lax.ppermute(value, axis, [(i, i ^ step) for i in range(size)])


def kernel_params(steps=0):
    return pltpu.CompilerParams(
        dimension_semantics=("arbitrary",) * steps if steps else None, vmem_limit_bytes=VMEM_BYTES
    )


IN_VMEM = pl.BlockSpec(memory_space=pltpu.VMEM)
IN_SMEM = pl.BlockSpec(memory_space=pltpu.SMEM)


def place_rows(result, plan, outs, lead, columns):
    for ref, pieces in zip(outs, plan):
        at = 0
        for start, count in pieces:
            rows = result[start : start + count].astype(ref.dtype)
            if lead is None:
                ref[at : at + count, columns] = rows
            else:
                ref[lead, at : at + count, columns] = rows
            at += count


def plan_rows(pieces):
    return sum(count for _, count in pieces)


def bring_kernel(place_ref, *refs):
    refs[-1][0] = place_ref[0]


def bring(place, weights):
    return pl.pallas_call(
        bring_kernel,
        in_specs=[IN_SMEM] + [IN_VMEM] * len(weights),
        out_specs=IN_SMEM,
        out_shape=jax.ShapeDtypeStruct((1,), jnp.int32),
        compiler_params=kernel_params(),
        cost_estimate=pl.CostEstimate(flops=0, bytes_accessed=0, transcendentals=0),
    )(place, *weights)


def project_kernel(ring, plan, by_unit, amount, place_ref, *refs):
    parts, refs = refs[: max(1, 2 * ring)], refs[max(1, 2 * ring) :]
    weights, masks, rows_ref, outs = refs[:amount], refs[amount : 2 * amount], refs[2 * amount], refs[2 * amount + 1 :]
    if not ring:
        rows_ref[...] = parts[0][...]
    else:
        place = place_ref[0]
        unit = parts[0].shape[0]
        for slot in range(ring):
            for source in range(ring):

                @pl.when((place ^ slot) == source)
                def _(slot=slot, source=source):
                    at = 2 * unit * slot
                    rows_ref[at : at + unit, :] = parts[source][...]
                    rows_ref[at + unit : at + 2 * unit, :] = parts[ring + source][...]

    rows = rows_ref[...]
    units = weights[0].shape[0] if by_unit else weights[0].shape[1]
    edge = block_edge(units)
    for lead, (weight, mask) in enumerate(zip(weights, masks)):
        for at in range(0, units, edge):
            columns = slice(at, at + edge)
            if by_unit:
                kept = masked(weight[columns, :], mask[at // BLOCK : (at + edge) // BLOCK, :])
                result = lax.dot_general(rows, kept, (((1,), (1,)), ((), ())), preferred_element_type=F32)
            else:
                kept = masked(weight[:, columns], mask[:, columns])
                result = jnp.dot(rows, kept, preferred_element_type=F32)
            place_rows(result, plan, outs, lead, columns)


def project(place, parts, weights, masks, plan, by_unit, weigh=0):
    ring = len(parts) // 2
    amount = len(weights)
    features = parts[0].shape[1]
    tokens = sum(part.shape[0] for part in parts)
    units = weights[0].shape[0] if by_unit else weights[0].shape[1]
    counts = [plan_rows(pieces) for pieces in plan]
    return pl.pallas_call(
        functools.partial(project_kernel, ring, plan, by_unit, amount),
        in_specs=[IN_SMEM] + [IN_VMEM] * (len(parts) + 2 * amount),
        out_specs=[IN_VMEM] * (1 + len(plan)),
        out_shape=[jax.ShapeDtypeStruct((tokens, features), BF16)]
        + [jax.ShapeDtypeStruct((amount, count, units), BF16) for count in counts],
        compiler_params=kernel_params(),
        cost_estimate=pl.CostEstimate(
            flops=2 * tokens * features * units * amount * weigh,
            bytes_accessed=2 * amount * features * units * weigh,
            transcendentals=0,
        ),
    )(place, *parts, *weights, *masks)


def contract_kernel(pieces, plan, by_unit, amount, *refs):
    parts, refs = refs[: len(pieces)], refs[len(pieces) :]
    weights, masks, rows_ref, outs = refs[:amount], refs[amount : 2 * amount], refs[2 * amount], refs[2 * amount + 1 :]
    at = 0
    for part, count in zip(parts, pieces):
        rows_ref[:, at : at + count, :] = part[...]
        at += count
    rows = [rows_ref[lead] for lead in range(amount)]
    features = weights[0].shape[1] if by_unit else weights[0].shape[0]
    edge = block_edge(features)
    for at in range(0, features, edge):
        columns = slice(at, at + edge)
        total = None
        for lead, (weight, mask) in enumerate(zip(weights, masks)):
            if by_unit:
                kept = masked(weight[:, columns], mask[:, columns])
                result = jnp.dot(rows[lead], kept, preferred_element_type=F32)
            else:
                kept = masked(weight[columns, :], mask[at // BLOCK : (at + edge) // BLOCK, :])
                result = lax.dot_general(rows[lead], kept, (((1,), (1,)), ((), ())), preferred_element_type=F32)
            total = result if total is None else total + result
        place_rows(total, plan, outs, None, columns)


def contract(parts, weights, masks, plan, types, by_unit, weigh=0):
    amount = len(weights)
    units = parts[0].shape[2]
    pieces = [part.shape[1] for part in parts]
    tokens = sum(pieces)
    features = weights[0].shape[1] if by_unit else weights[0].shape[0]
    counts = [plan_rows(piece) for piece in plan]
    return pl.pallas_call(
        functools.partial(contract_kernel, pieces, plan, by_unit, amount),
        in_specs=[IN_VMEM] * (len(parts) + 2 * amount),
        out_specs=[IN_VMEM] * (1 + len(plan)),
        out_shape=[jax.ShapeDtypeStruct((amount, tokens, units), BF16)]
        + [jax.ShapeDtypeStruct((count, features), kind) for count, kind in zip(counts, types)],
        compiler_params=kernel_params(),
        cost_estimate=pl.CostEstimate(
            flops=2 * tokens * features * units * amount * weigh,
            bytes_accessed=2 * amount * features * units * weigh,
            transcendentals=0,
        ),
    )(*parts, *weights, *masks)


def outer_kernel(left_ref, right_ref, *refs):
    amount = right_ref.shape[0]
    masks, outs = refs[:amount], refs[amount:]
    edge = outs[0].shape[0]
    left = left_ref[:, pl.ds(pl.multiple_of(pl.program_id(0) * edge, edge), edge)]
    for lead in range(amount):
        result = lax.dot_general(left, right_ref[lead], (((0,), (0,)), ((), ())), preferred_element_type=F32)
        outs[lead][...] = masked(result, masks[lead][0].astype(F32))


def outer(left, right, masks):
    tokens, rows = left.shape
    amount, _, width = right.shape
    edge = block_edge(rows)
    return pl.pallas_call(
        outer_kernel,
        grid=(rows // edge,),
        in_specs=[IN_VMEM, IN_VMEM] + [pl.BlockSpec((1, edge // BLOCK, width), lambda j: (j, 0, 0))] * amount,
        out_specs=[pl.BlockSpec((edge, width), lambda j: (j, 0))] * amount,
        out_shape=[jax.ShapeDtypeStruct((rows, width), F32)] * amount,
        compiler_params=kernel_params(1),
        cost_estimate=pl.CostEstimate(
            flops=0, bytes_accessed=0, transcendentals=0
        ),
    )(left, right, *masks)


def owner_kernel(count, place_ref, own_ref, got_ref, *refs):
    factors, outs, sums = refs[:-count], refs[-count:], ()
    if factors:
        factors, outs, sums = refs[:count], refs[count : 2 * count], refs[2 * count :]
    unit = outs[0].shape[0]
    place = place_ref[0]
    down = None
    for step in range(count):
        rows = pl.ds(pl.multiple_of((place ^ step) * unit, 16), unit)
        part = own_ref[rows, :] + got_ref[rows, :].astype(F32)
        outs[step][...] = part.astype(outs[step].dtype)
        if factors:
            product = part * factors[step][...].astype(F32)
            across = jnp.sum(product, axis=1, keepdims=True)
            sums[0][step * unit : (step + 1) * unit, :] = jnp.broadcast_to(across, (unit, sums[0].shape[1]))
            step_down = jnp.sum(product, axis=0, keepdims=True)
            down = step_down if down is None else down + step_down
    if factors:
        sums[1][...] = down


def owner(place, own, got, count, factors=()):
    total, features = own.shape
    unit = total // count
    outs = [jax.ShapeDtypeStruct((unit, features), F32 if step == 0 else BF16) for step in range(count)]
    if factors:
        outs += [jax.ShapeDtypeStruct((total, 128), F32), jax.ShapeDtypeStruct((1, features), F32)]
    return pl.pallas_call(
        functools.partial(owner_kernel, count),
        in_specs=[IN_SMEM] + [IN_VMEM] * (2 + len(factors)),
        out_specs=[IN_VMEM] * len(outs),
        out_shape=outs,
        compiler_params=kernel_params(),
    )(place, own, got, *factors)


def activation(gate, up_value, hidden_grad):
    sigmoid_gate = 1.0 / (1.0 + jnp.exp(-gate))
    scaled = gate * sigmoid_gate
    hidden = scaled * up_value
    gate_grad = hidden_grad * up_value * sigmoid_gate * (1.0 + gate * (1.0 - sigmoid_gate))
    up_grad = hidden_grad * scaled
    return hidden, gate_grad, up_grad


def activate_kernel(*refs):
    pair, one, (hidden_ref, grads_ref) = refs[:5], refs[5:10], refs[10:]
    half = pair[3].shape[1]
    for second in (False, True):
        at = half if second else 0
        rows = slice(at, at + half)

        def summed(parts, lead):
            own, first_x, first_y, last_y, last_x = parts
            first, last = (first_y, last_x) if second else (first_x, last_y)
            return own[lead, rows].astype(F32) + first[lead, half:].astype(F32) + last[lead].astype(F32)

        results = activation(summed(pair, 0), summed(pair, 1), summed(one, 0))
        hidden_ref[0, rows] = results[0].astype(BF16)
        grads_ref[0, rows] = results[1].astype(BF16)
        grads_ref[1, rows] = results[2].astype(BF16)


def activate(pair, one):
    _, share, units = pair[0].shape
    edge = block_edge(units)
    spec = lambda array: pl.BlockSpec(array.shape[:2] + (edge,), lambda j: (0, 0, j))
    outs = [jax.ShapeDtypeStruct((amount, share, units), BF16) for amount in (1, 2)]
    return pl.pallas_call(
        activate_kernel,
        grid=(units // edge,),
        in_specs=[spec(array) for array in pair + one],
        out_specs=[spec(array) for array in outs],
        out_shape=outs,
        compiler_params=kernel_params(1),
    )(*pair, *one)


def widen(keep):
    return jnp.repeat(keep, BLOCK, axis=1).astype(BF16)


def widen_grouped(keep):
    together = block_edge(keep.shape[0] * BLOCK) // BLOCK
    return widen(keep).reshape(-1, together, keep.shape[1] * BLOCK)


def finish(token_f, inv_rms, norm_gain, normed_grad, inner_sum, gain_sum):
    grad_gain = gain_sum(jnp.sum(normed_grad * token_f * inv_rms, axis=0))
    inner_dot = inner_sum(jnp.sum(norm_gain * normed_grad * token_f, axis=1))
    width = norm_gain.shape[0] * lax.axis_size("row")
    grad_tokens = (
        inv_rms * norm_gain * normed_grad
        - token_f * inv_rms * inv_rms * inv_rms * inner_dot[:, None] / width
    )
    return grad_tokens, grad_gain


def ordered(*groups):
    return lax.optimization_barrier(groups)


def exchange_device(
    tokens, norm_gain, gate_weight, up_weight, down_weight, gate_keep, up_keep, down_keep, cotangent
):
    rows, cols = 4, 4
    unit, features = tokens.shape
    place = lax.axis_index("row")
    place_arg = place.astype(jnp.int32).reshape(1)

    def core_swap(value):
        return swap(value, "dp", 2, 1)

    def row_swap(value, step):
        return swap(value, "row", rows, step)

    def level_swaps(parts):
        return [swap(part, "col", cols, step + 1) for step, part in enumerate(parts)]

    def balanced(value, got):
        return (value + got[0]) + (got[1] + got[2])

    def row_sum(value):
        value = value + row_swap(value, 1)
        return value + row_swap(value, 2)

    def sum_first(x_first, y_first):
        return ordered(row_swap(x_first, 1), row_swap(y_first, 2))

    def sum_middle(x_keep, y_keep, got_x, got_y):
        half = x_keep.shape[1]
        add = lambda a, b: (a.astype(F32) + b[:, :half].astype(F32)).astype(BF16)
        return add(y_keep, got_x), add(x_keep, got_y)

    def sum_last(for_y, for_x):
        return ordered(row_swap(for_y, 2), row_swap(for_x, 1))

    def gather_first(share):
        return ordered(row_swap(share, 1), row_swap(share, 2))

    def gather_middle(got_x, got_y):
        return got_y[:, :unit], got_x[:, unit:]

    def gather_last(for_x, for_y):
        return ordered(row_swap(for_x, 1), row_swap(for_y, 2))

    def owner_total(kept, got):
        return balanced(kept, [part.astype(F32) for part in got])

    def rows_of(slot, second):
        return (2 * unit * slot + (unit if second else 0), unit)

    first_plan = [
        [rows_of(3, False), rows_of(1, False)],
        [rows_of(3, True), rows_of(2, True)],
        [rows_of(1, True)],
        [rows_of(2, False)],
        [(0, 2 * unit)],
    ]
    last_plan = [[rows_of(slot, False) for slot in range(rows)], [rows_of(slot, True) for slot in range(rows)]]

    token_f = tokens.astype(F32)
    squares = jnp.sum(token_f * token_f, axis=1)
    cot_far = level_swaps([cotangent] * 3)
    inv_rms = lax.rsqrt(row_sum(squares)[:, None] / (features * rows) + 1e-05)
    normed = (token_f * inv_rms * norm_gain).astype(BF16)
    gate_mask, up_mask, down_mask = widen(gate_keep), widen(up_keep), widen(down_keep)
    gate_groups, up_groups, down_groups = widen_grouped(gate_keep), widen_grouped(up_keep), widen_grouped(down_keep)
    cot_core, normed_core = core_swap(cotangent), core_swap(normed)
    masks = [gate_mask, up_mask, down_mask, gate_groups, up_groups, down_groups]
    place, place_arg, masks = ordered(place, place_arg, masks)
    gate_mask, up_mask, down_mask, gate_groups, up_groups, down_groups = masks
    place_arg = bring(place_arg, [down_weight, gate_weight, up_weight])
    cot_far, cot_core, normed, normed_core, place_arg = ordered(cot_far, cot_core, normed, normed_core, place_arg)
    cot_own = [cotangent, *cot_far]
    cot_other = [cot_core] + [core_swap(part) for part in cot_far]

    normed_far = level_swaps([normed] * 3)
    seen_cot, *one_parts = project(
        place_arg, cot_own + cot_other, [down_weight], [down_mask], first_plan, True
    )
    one_x, one_y = sum_first(*one_parts[:2])
    normed_far, one_keep = ordered(normed_far, one_parts[2:])
    normed_own = [normed, *normed_far]
    normed_other = [normed_core] + [core_swap(part) for part in normed_far]

    seen_rows, *pair_parts = project(place_arg, normed_own + normed_other, [gate_weight, up_weight], [gate_mask, up_mask], first_plan, False)
    one_x, one_y, pair_parts = ordered(one_x, one_y, pair_parts)
    pair_x, pair_y = sum_first(*pair_parts[:2])
    one_last = sum_last(*sum_middle(*one_keep[:2], one_x, one_y))
    pair_last = sum_last(*sum_middle(*pair_parts[2:4], pair_x, pair_y))
    hidden_share, grads_share = activate(
        [pair_parts[4], pair_x, pair_y, *pair_last], [one_keep[2], one_x, one_y, *one_last]
    )

    hidden_x, hidden_y = gather_first(hidden_share)
    hidden_middle = gather_middle(hidden_x, hidden_y)
    grads_share, hidden_middle = ordered(grads_share, hidden_middle)
    grads_x, grads_y = gather_first(grads_share)
    hidden_last = gather_last(*hidden_middle)
    hidden, branch_own, branch_other = contract(
        [hidden_share, hidden_x, hidden_y, *hidden_last], [down_weight], [down_mask], last_plan, (F32, BF16), True, 10
    )
    grads_x, grads_y, branch_own, branch_other = ordered(grads_x, grads_y, branch_own, branch_other)
    branch_got = core_swap(branch_other)
    grads_middle = gather_middle(grads_x, grads_y)
    grads_last = gather_last(*grads_middle)
    branch_kept, *branch_parts = owner(place_arg, branch_own, branch_got, cols)
    branch_far = level_swaps(branch_parts)
    hidden, grads_middle = ordered(hidden, grads_middle)
    (grad_down,) = outer(hidden[0], seen_cot[None], [down_groups])
    grads_last, grad_down = ordered(grads_last, grad_down)

    grads, normed_mine, normed_theirs = contract(
        [grads_share, grads_x, grads_y, *grads_last], [gate_weight, up_weight], [gate_mask, up_mask], last_plan, (F32, BF16), False
    )
    branch_far, normed_mine, normed_theirs = ordered(branch_far, normed_mine, normed_theirs)

    kept, *parts, across, down_sum = owner(place_arg, normed_mine, core_swap(normed_theirs), cols, normed_own)
    grads, parts, across, down_sum = ordered(grads, parts, across, down_sum)
    far = level_swaps(parts)
    across_x = across + row_swap(across, 1)
    down_both = down_sum + core_swap(down_sum)
    across_x, down_both, grads = ordered(across_x, down_both, grads)
    across_row = across_x + row_swap(across_x, 2)
    sums = [
        jnp.concatenate([across_row[step * unit : (step + 1) * unit], down_both.reshape(-1, 128)])
        for step in range(cols)
    ]
    grads, sums = ordered(grads, sums)
    sums_far = level_swaps(sums[1:])
    grad_gate, grad_up = outer(seen_rows, grads, [gate_groups, up_groups])
    far, sums_far, grad_gate, grad_up = ordered(far, sums_far, grad_gate, grad_up)
    sums_total = balanced(sums[0], sums_far)
    branch = owner_total(branch_kept, branch_far).astype(BF16)
    normed_grad = owner_total(kept, far)
    grad_gain = sums_total[unit:].reshape(features) / norm_gain
    grad_tokens = (
        inv_rms * norm_gain * normed_grad - token_f * inv_rms * inv_rms * sums_total[:unit, :1] / (features * rows)
    )
    return (branch, grad_tokens, grad_gain, grad_gate, grad_up, grad_down)


def general_device(
    tokens, norm_gain, gate_weight, up_weight, down_weight, gate_keep, up_keep, down_keep, cotangent
):
    owners = ("dp", "col")
    features = tokens.shape[1]
    place_arg = jnp.zeros((1,), jnp.int32)
    token_f = tokens.astype(F32)
    square = lax.psum(jnp.sum(token_f * token_f, axis=1), "row")
    inv_rms = lax.rsqrt(square[:, None] / (features * lax.axis_size("row")) + 1e-05)
    normed = (token_f * inv_rms * norm_gain).astype(BF16)
    gate_mask, up_mask, down_mask = widen(gate_keep), widen(up_keep), widen(down_keep)
    gate_groups, up_groups, down_groups = widen_grouped(gate_keep), widen_grouped(up_keep), widen_grouped(down_keep)
    seen_cot = lax.all_gather(cotangent, owners, axis=0, tiled=True)
    seen_rows = lax.all_gather(normed, owners, axis=0, tiled=True)
    plan = [[(0, seen_cot.shape[0])]]

    def share(value):
        return lax.psum_scatter(value.astype(F32), "row", scatter_dimension=1, tiled=True)

    def collect(value):
        return lax.all_gather(value.astype(BF16), "row", axis=1, tiled=True)

    def owner_sum(value):
        return lax.psum_scatter(value, owners, scatter_dimension=0, tiled=True)

    _, one = project(place_arg, [seen_cot], [down_weight], [down_mask], plan, True)
    _, pair = project(place_arg, [seen_rows], [gate_weight, up_weight], [gate_mask, up_mask], plan, False)
    pair = share(pair)
    hidden, gate_grad, up_grad = activation(pair[0], pair[1], share(one)[0])
    hidden, branch = contract([collect(hidden[None])], [down_weight], [down_mask], plan, (F32,), True)
    branch = owner_sum(branch).astype(BF16)
    grads, normed_grad = contract(
        [collect(jnp.stack([gate_grad, up_grad]))], [gate_weight, up_weight], [gate_mask, up_mask], plan, (F32,), False
    )
    normed_grad = owner_sum(normed_grad)
    (grad_down,) = outer(hidden[0], seen_cot[None], [down_groups])
    grad_gate, grad_up = outer(seen_rows, grads, [gate_groups, up_groups])
    grad_tokens, grad_gain = finish(
        token_f,
        inv_rms,
        norm_gain,
        normed_grad,
        lambda value: lax.psum(value, "row"),
        lambda value: lax.psum(value, owners),
    )
    return (branch, grad_tokens, grad_gain, grad_gate, grad_up, grad_down)


def solution(mesh):
    split = P(("dp", "col"), "row")
    turned = P("row", ("dp", "col"))
    sizes = (mesh.shape["dp"], mesh.shape["row"], mesh.shape["col"])
    on_device = exchange_device if sizes == (2, 4, 4) else general_device
    return jax.shard_map(
        on_device,
        mesh=mesh,
        in_specs=(split, P("row"), turned, turned, split, turned, turned, split, split),
        out_specs=(split, split, P("row"), turned, turned, split),
        check_vma=False,
    )
```

```python
import functools
import jax
import jax.numpy as jnp
from jax import lax
from jax.experimental import pallas as pl
from jax.experimental.pallas import tpu as pltpu
from jax.sharding import PartitionSpec as P

BLOCK = 128
VMEM_BYTES = 10 * 1024 * 1024
BF16 = jnp.bfloat16
F32 = jnp.float32


def block_edge(extent):
    return 256 if extent % 256 == 0 else 128


def masked(weight, mask):
    groups, width = mask.shape
    shaped = weight.reshape(groups, BLOCK, width) * mask[:, None, :]
    return shaped.reshape(groups * BLOCK, width)


def swap(value, axis, size, step):
    return lax.ppermute(value, axis, [(i, i ^ step) for i in range(size)])


def kernel_params(steps=0):
    return pltpu.CompilerParams(
        dimension_semantics=("arbitrary",) * steps if steps else None, vmem_limit_bytes=VMEM_BYTES
    )


IN_VMEM = pl.BlockSpec(memory_space=pltpu.VMEM)
IN_SMEM = pl.BlockSpec(memory_space=pltpu.SMEM)


def place_rows(result, plan, outs, lead, columns):
    for ref, pieces in zip(outs, plan):
        at = 0
        for start, count in pieces:
            rows = result[start : start + count].astype(ref.dtype)
            if lead is None:
                ref[at : at + count, columns] = rows
            else:
                ref[lead, at : at + count, columns] = rows
            at += count


def plan_rows(pieces):
    return sum(count for _, count in pieces)


def bring_kernel(place_ref, *refs):
    refs[-1][0] = place_ref[0]


def bring(place, weights):
    return pl.pallas_call(
        bring_kernel,
        in_specs=[IN_SMEM] + [IN_VMEM] * len(weights),
        out_specs=IN_SMEM,
        out_shape=jax.ShapeDtypeStruct((1,), jnp.int32),
        compiler_params=kernel_params(),
        cost_estimate=pl.CostEstimate(flops=0, bytes_accessed=0, transcendentals=0),
    )(place, *weights)


def project_kernel(ring, plan, by_unit, amount, place_ref, *refs):
    parts, refs = refs[: max(1, 2 * ring)], refs[max(1, 2 * ring) :]
    weights, masks, rows_ref, outs = refs[:amount], refs[amount : 2 * amount], refs[2 * amount], refs[2 * amount + 1 :]
    if not ring:
        rows_ref[...] = parts[0][...]
    else:
        place = place_ref[0]
        unit = parts[0].shape[0]
        for slot in range(ring):
            for source in range(ring):

                @pl.when((place ^ slot) == source)
                def _(slot=slot, source=source):
                    at = 2 * unit * slot
                    rows_ref[at : at + unit, :] = parts[source][...]
                    rows_ref[at + unit : at + 2 * unit, :] = parts[ring + source][...]

    rows = rows_ref[...]
    units = weights[0].shape[0] if by_unit else weights[0].shape[1]
    edge = block_edge(units)
    for lead, (weight, mask) in enumerate(zip(weights, masks)):
        for at in range(0, units, edge):
            columns = slice(at, at + edge)
            if by_unit:
                kept = masked(weight[columns, :], mask[at // BLOCK : (at + edge) // BLOCK, :])
                result = lax.dot_general(rows, kept, (((1,), (1,)), ((), ())), preferred_element_type=F32)
            else:
                kept = masked(weight[:, columns], mask[:, columns])
                result = jnp.dot(rows, kept, preferred_element_type=F32)
            place_rows(result, plan, outs, lead, columns)


def project(place, parts, weights, masks, plan, by_unit, weigh=0):
    ring = len(parts) // 2
    amount = len(weights)
    features = parts[0].shape[1]
    tokens = sum(part.shape[0] for part in parts)
    units = weights[0].shape[0] if by_unit else weights[0].shape[1]
    counts = [plan_rows(pieces) for pieces in plan]
    return pl.pallas_call(
        functools.partial(project_kernel, ring, plan, by_unit, amount),
        in_specs=[IN_SMEM] + [IN_VMEM] * (len(parts) + 2 * amount),
        out_specs=[IN_VMEM] * (1 + len(plan)),
        out_shape=[jax.ShapeDtypeStruct((tokens, features), BF16)]
        + [jax.ShapeDtypeStruct((amount, count, units), BF16) for count in counts],
        compiler_params=kernel_params(),
        cost_estimate=pl.CostEstimate(
            flops=2 * tokens * features * units * amount * weigh,
            bytes_accessed=2 * amount * features * units * weigh,
            transcendentals=0,
        ),
    )(place, *parts, *weights, *masks)


def contract_kernel(pieces, plan, by_unit, amount, *refs):
    parts, refs = refs[: len(pieces)], refs[len(pieces) :]
    weights, masks, rows_ref, outs = refs[:amount], refs[amount : 2 * amount], refs[2 * amount], refs[2 * amount + 1 :]
    at = 0
    for part, count in zip(parts, pieces):
        rows_ref[:, at : at + count, :] = part[...]
        at += count
    rows = [rows_ref[lead] for lead in range(amount)]
    features = weights[0].shape[1] if by_unit else weights[0].shape[0]
    edge = block_edge(features)
    for at in range(0, features, edge):
        columns = slice(at, at + edge)
        total = None
        for lead, (weight, mask) in enumerate(zip(weights, masks)):
            if by_unit:
                kept = masked(weight[:, columns], mask[:, columns])
                result = jnp.dot(rows[lead], kept, preferred_element_type=F32)
            else:
                kept = masked(weight[columns, :], mask[at // BLOCK : (at + edge) // BLOCK, :])
                result = lax.dot_general(rows[lead], kept, (((1,), (1,)), ((), ())), preferred_element_type=F32)
            total = result if total is None else total + result
        place_rows(total, plan, outs, None, columns)


def contract(parts, weights, masks, plan, types, by_unit, weigh=0):
    amount = len(weights)
    units = parts[0].shape[2]
    pieces = [part.shape[1] for part in parts]
    tokens = sum(pieces)
    features = weights[0].shape[1] if by_unit else weights[0].shape[0]
    counts = [plan_rows(piece) for piece in plan]
    return pl.pallas_call(
        functools.partial(contract_kernel, pieces, plan, by_unit, amount),
        in_specs=[IN_VMEM] * (len(parts) + 2 * amount),
        out_specs=[IN_VMEM] * (1 + len(plan)),
        out_shape=[jax.ShapeDtypeStruct((amount, tokens, units), BF16)]
        + [jax.ShapeDtypeStruct((count, features), kind) for count, kind in zip(counts, types)],
        compiler_params=kernel_params(),
        cost_estimate=pl.CostEstimate(
            flops=2 * tokens * features * units * amount * weigh,
            bytes_accessed=2 * amount * features * units * weigh,
            transcendentals=0,
        ),
    )(*parts, *weights, *masks)


def outer_kernel(left_ref, right_ref, *refs):
    amount = right_ref.shape[0]
    masks, outs = refs[:amount], refs[amount:]
    edge = outs[0].shape[0]
    left = left_ref[:, pl.ds(pl.multiple_of(pl.program_id(0) * edge, edge), edge)]
    for lead in range(amount):
        result = lax.dot_general(left, right_ref[lead], (((0,), (0,)), ((), ())), preferred_element_type=F32)
        outs[lead][...] = masked(result, masks[lead][0].astype(F32))


def outer(left, right, masks):
    tokens, rows = left.shape
    amount, _, width = right.shape
    edge = block_edge(rows)
    return pl.pallas_call(
        outer_kernel,
        grid=(rows // edge,),
        in_specs=[IN_VMEM, IN_VMEM] + [pl.BlockSpec((1, edge // BLOCK, width), lambda j: (j, 0, 0))] * amount,
        out_specs=[pl.BlockSpec((edge, width), lambda j: (j, 0))] * amount,
        out_shape=[jax.ShapeDtypeStruct((rows, width), F32)] * amount,
        compiler_params=kernel_params(1),
        cost_estimate=pl.CostEstimate(
            flops=0, bytes_accessed=0, transcendentals=0
        ),
    )(left, right, *masks)


def owner_kernel(count, place_ref, own_ref, got_ref, *refs):
    factors = refs[:count] if len(refs) > count else ()
    outs = refs[len(factors) : len(factors) + count]
    unit = outs[0].shape[0]
    place = place_ref[0]
    down = None
    for step in range(count):
        rows = pl.ds(pl.multiple_of((place ^ step) * unit, 16), unit)
        part = own_ref[rows, :] + got_ref[rows, :].astype(F32)
        outs[step][...] = part.astype(outs[step].dtype)
        if factors:
            step_down = jnp.sum(part * factors[step][...].astype(F32), axis=0, keepdims=True)
            down = step_down if down is None else down + step_down
    if factors:
        refs[-1][...] = down


def owner(place, own, got, count, factors=()):
    total, features = own.shape
    unit = total // count
    outs = [jax.ShapeDtypeStruct((unit, features), F32 if step == 0 else BF16) for step in range(count)]
    if factors:
        outs += [jax.ShapeDtypeStruct((1, features), F32)]
    return pl.pallas_call(
        functools.partial(owner_kernel, count),
        in_specs=[IN_SMEM] + [IN_VMEM] * (2 + len(factors)),
        out_specs=[IN_VMEM] * len(outs),
        out_shape=outs,
        compiler_params=kernel_params(),
    )(place, own, got, *factors)


def activation(gate, up_value, hidden_grad):
    sigmoid_gate = 1.0 / (1.0 + jnp.exp(-gate))
    scaled = gate * sigmoid_gate
    hidden = scaled * up_value
    gate_grad = hidden_grad * up_value * sigmoid_gate * (1.0 + gate * (1.0 - sigmoid_gate))
    up_grad = hidden_grad * scaled
    return hidden, gate_grad, up_grad


def activate_kernel(*refs):
    pair, one, (hidden_ref, grads_ref, sums_ref, held_ref) = refs[:5], refs[5:10], refs[10:]
    half = pair[3].shape[1]
    for second in (False, True):
        at = half if second else 0
        rows = slice(at, at + half)

        def summed(parts, lead):
            own, first_x, first_y, last_y, last_x = parts
            first, last = (first_y, last_x) if second else (first_x, last_y)
            return own[lead, rows].astype(F32) + first[lead, half:].astype(F32) + last[lead].astype(F32)

        gate, up_value = summed(pair, 0), summed(pair, 1)
        hidden, *grads = activation(gate, up_value, summed(one, 0))
        hidden_ref[0, rows] = hidden.astype(BF16)
        products = 0.0
        for lead, (grad, value) in enumerate(zip(grads, (gate, up_value))):
            rounded = grad.astype(BF16)
            grads_ref[lead, rows] = rounded
            products = products + rounded.astype(F32) * value

        @pl.when(pl.program_id(0) == 0)
        def _():
            held_ref[rows] = products

        @pl.when(pl.program_id(0) > 0)
        def _():
            held_ref[rows] = held_ref[rows] + products

    @pl.when(pl.program_id(0) == pl.num_programs(0) - 1)
    def _():
        sums_ref[...] = jnp.broadcast_to(jnp.sum(held_ref[...], axis=1, keepdims=True), sums_ref.shape)


def activate(pair, one):
    _, share, units = pair[0].shape
    edge = block_edge(units)
    spec = lambda array: pl.BlockSpec(array.shape[:2] + (edge,), lambda j: (0, 0, j))
    outs = [jax.ShapeDtypeStruct((amount, share, units), BF16) for amount in (1, 2)]
    return pl.pallas_call(
        activate_kernel,
        grid=(units // edge,),
        in_specs=[spec(array) for array in pair + one],
        out_specs=[spec(array) for array in outs] + [pl.BlockSpec((share, BLOCK), lambda j: (0, 0))],
        out_shape=outs + [jax.ShapeDtypeStruct((share, BLOCK), F32)],
        scratch_shapes=[pltpu.VMEM((share, edge), F32)],
        compiler_params=kernel_params(1),
    )(*pair, *one)


def widen(keep):
    return jnp.repeat(keep, BLOCK, axis=1).astype(BF16)


def widen_grouped(keep):
    together = block_edge(keep.shape[0] * BLOCK) // BLOCK
    return widen(keep).reshape(-1, together, keep.shape[1] * BLOCK)


def finish(token_f, inv_rms, norm_gain, normed_grad, inner_sum, gain_sum):
    grad_gain = gain_sum(jnp.sum(normed_grad * token_f * inv_rms, axis=0))
    inner_dot = inner_sum(jnp.sum(norm_gain * normed_grad * token_f, axis=1))
    width = norm_gain.shape[0] * lax.axis_size("row")
    grad_tokens = (
        inv_rms * norm_gain * normed_grad
        - token_f * inv_rms * inv_rms * inv_rms * inner_dot[:, None] / width
    )
    return grad_tokens, grad_gain


def ordered(*groups):
    return lax.optimization_barrier(groups)


def exchange_device(
    tokens, norm_gain, gate_weight, up_weight, down_weight, gate_keep, up_keep, down_keep, cotangent
):
    rows, cols = 4, 4
    unit, features = tokens.shape
    place = lax.axis_index("row")
    place_arg = place.astype(jnp.int32).reshape(1)

    def core_swap(value):
        return swap(value, "dp", 2, 1)

    def row_swap(value, step):
        return swap(value, "row", rows, step)

    def level_swaps(parts):
        return [swap(part, "col", cols, step + 1) for step, part in enumerate(parts)]

    def balanced(value, got):
        return (value + got[0]) + (got[1] + got[2])

    def row_sum(value):
        value = value + row_swap(value, 1)
        return value + row_swap(value, 2)

    def sum_first(x_first, y_first):
        return ordered(row_swap(x_first, 1), row_swap(y_first, 2))

    def sum_middle(x_keep, y_keep, got_x, got_y):
        half = x_keep.shape[1]
        add = lambda a, b: (a.astype(F32) + b[:, :half].astype(F32)).astype(BF16)
        return add(y_keep, got_x), add(x_keep, got_y)

    def sum_last(for_y, for_x):
        return ordered(row_swap(for_y, 2), row_swap(for_x, 1))

    def gather_first(share):
        return ordered(row_swap(share, 1), row_swap(share, 2))

    def gather_middle(got_x, got_y):
        return got_y[:, :unit], got_x[:, unit:]

    def gather_last(for_x, for_y):
        return ordered(row_swap(for_x, 1), row_swap(for_y, 2))

    def owner_total(kept, got):
        return balanced(kept, [part.astype(F32) for part in got])

    def rows_of(slot, second):
        return (2 * unit * slot + (unit if second else 0), unit)

    first_plan = [
        [rows_of(3, False), rows_of(1, False)],
        [rows_of(3, True), rows_of(2, True)],
        [rows_of(1, True)],
        [rows_of(2, False)],
        [(0, 2 * unit)],
    ]
    last_plan = [[rows_of(slot, False) for slot in range(rows)], [rows_of(slot, True) for slot in range(rows)]]

    token_f = tokens.astype(F32)
    squares = jnp.sum(token_f * token_f, axis=1)
    cot_far = level_swaps([cotangent] * 3)
    inv_rms = lax.rsqrt(row_sum(squares)[:, None] / (features * rows) + 1e-05)
    normed = (token_f * inv_rms * norm_gain).astype(BF16)
    gate_mask, up_mask, down_mask = widen(gate_keep), widen(up_keep), widen(down_keep)
    gate_groups, up_groups, down_groups = widen_grouped(gate_keep), widen_grouped(up_keep), widen_grouped(down_keep)
    cot_core, normed_core = core_swap(cotangent), core_swap(normed)
    masks = [gate_mask, up_mask, down_mask, gate_groups, up_groups, down_groups]
    place, place_arg, masks = ordered(place, place_arg, masks)
    gate_mask, up_mask, down_mask, gate_groups, up_groups, down_groups = masks
    place_arg = bring(place_arg, [down_weight, gate_weight, up_weight])
    cot_far, cot_core, normed, normed_core, place_arg = ordered(cot_far, cot_core, normed, normed_core, place_arg)
    cot_own = [cotangent, *cot_far]
    cot_other = [cot_core] + [core_swap(part) for part in cot_far]

    normed_far = level_swaps([normed] * 3)
    seen_cot, *one_parts = project(
        place_arg, cot_own + cot_other, [down_weight], [down_mask], first_plan, True
    )
    one_x, one_y = sum_first(*one_parts[:2])
    normed_far, one_keep = ordered(normed_far, one_parts[2:])
    normed_own = [normed, *normed_far]
    normed_other = [normed_core] + [core_swap(part) for part in normed_far]

    seen_rows, *pair_parts = project(place_arg, normed_own + normed_other, [gate_weight, up_weight], [gate_mask, up_mask], first_plan, False)
    one_x, one_y, pair_parts = ordered(one_x, one_y, pair_parts)
    pair_x, pair_y = sum_first(*pair_parts[:2])
    one_last = sum_last(*sum_middle(*one_keep[:2], one_x, one_y))
    pair_last = sum_last(*sum_middle(*pair_parts[2:4], pair_x, pair_y))
    hidden_share, grads_share, inner_share = activate(
        [pair_parts[4], pair_x, pair_y, *pair_last], [one_keep[2], one_x, one_y, *one_last]
    )

    hidden_x, hidden_y = gather_first(hidden_share)
    hidden_middle = gather_middle(hidden_x, hidden_y)
    grads_share, hidden_middle = ordered(grads_share, hidden_middle)
    grads_x, grads_y = gather_first(grads_share)
    hidden_last = gather_last(*hidden_middle)
    hidden, branch_own, branch_other = contract(
        [hidden_share, hidden_x, hidden_y, *hidden_last], [down_weight], [down_mask], last_plan, (F32, BF16), True, 10
    )
    inner_share, branch_own = ordered(inner_share, branch_own)
    inner = inner_share[:unit] + core_swap(inner_share[unit:])
    to_owner = [(r * cols + z, r * cols + (z ^ r)) for r in range(rows) for z in range(cols)]
    inner = lax.ppermute(inner, ("row", "col"), to_owner)
    grads_x, grads_y, branch_own, branch_other, inner = ordered(grads_x, grads_y, branch_own, branch_other, inner)
    branch_got = core_swap(branch_other)
    grads_middle = gather_middle(grads_x, grads_y)
    grads_last = gather_last(*grads_middle)
    branch_kept, *branch_parts = owner(place_arg, branch_own, branch_got, cols)
    branch_far = level_swaps(branch_parts)
    hidden, grads_middle = ordered(hidden, grads_middle)
    (grad_down,) = outer(hidden[0], seen_cot[None], [down_groups])
    grads_last, grad_down = ordered(grads_last, grad_down)

    grads, normed_mine, normed_theirs = contract(
        [grads_share, grads_x, grads_y, *grads_last], [gate_weight, up_weight], [gate_mask, up_mask], last_plan, (F32, BF16), False
    )
    branch_far, normed_mine, normed_theirs = ordered(branch_far, normed_mine, normed_theirs)

    kept, *parts, down_sum = owner(place_arg, normed_mine, core_swap(normed_theirs), cols, normed_own)
    grads, parts, down_sum, inner = ordered(grads, parts, down_sum, inner)
    far = level_swaps(parts)
    down_pair = down_sum + swap(down_sum, "col", cols, 1)
    inner_pair = inner + row_swap(inner, 1)
    grads, down_pair, inner_pair = ordered(grads, down_pair, inner_pair)
    down_got = swap(down_pair, "col", cols, 2)
    inner_got = row_swap(inner_pair, 2)
    grad_gate, grad_up = outer(seen_rows, grads, [gate_groups, up_groups])
    far, down_got, inner_got, grad_gate, grad_up = ordered(far, down_got, inner_got, grad_gate, grad_up)
    inner = inner_pair + inner_got
    down_levels = down_pair + down_got
    down_total = down_levels + core_swap(down_levels)
    branch = owner_total(branch_kept, branch_far).astype(BF16)
    normed_grad = owner_total(kept, far)
    grad_gain = down_total.reshape(features) / norm_gain
    grad_tokens = (
        inv_rms * norm_gain * normed_grad - token_f * inv_rms * inv_rms * inner[:, :1] / (features * rows)
    )
    return (branch, grad_tokens, grad_gain, grad_gate, grad_up, grad_down)


def general_device(
    tokens, norm_gain, gate_weight, up_weight, down_weight, gate_keep, up_keep, down_keep, cotangent
):
    owners = ("dp", "col")
    features = tokens.shape[1]
    place_arg = jnp.zeros((1,), jnp.int32)
    token_f = tokens.astype(F32)
    square = lax.psum(jnp.sum(token_f * token_f, axis=1), "row")
    inv_rms = lax.rsqrt(square[:, None] / (features * lax.axis_size("row")) + 1e-05)
    normed = (token_f * inv_rms * norm_gain).astype(BF16)
    gate_mask, up_mask, down_mask = widen(gate_keep), widen(up_keep), widen(down_keep)
    gate_groups, up_groups, down_groups = widen_grouped(gate_keep), widen_grouped(up_keep), widen_grouped(down_keep)
    seen_cot = lax.all_gather(cotangent, owners, axis=0, tiled=True)
    seen_rows = lax.all_gather(normed, owners, axis=0, tiled=True)
    plan = [[(0, seen_cot.shape[0])]]

    def share(value):
        return lax.psum_scatter(value.astype(F32), "row", scatter_dimension=1, tiled=True)

    def collect(value):
        return lax.all_gather(value.astype(BF16), "row", axis=1, tiled=True)

    def owner_sum(value):
        return lax.psum_scatter(value, owners, scatter_dimension=0, tiled=True)

    _, one = project(place_arg, [seen_cot], [down_weight], [down_mask], plan, True)
    _, pair = project(place_arg, [seen_rows], [gate_weight, up_weight], [gate_mask, up_mask], plan, False)
    pair = share(pair)
    hidden, gate_grad, up_grad = activation(pair[0], pair[1], share(one)[0])
    hidden, branch = contract([collect(hidden[None])], [down_weight], [down_mask], plan, (F32,), True)
    branch = owner_sum(branch).astype(BF16)
    grads, normed_grad = contract(
        [collect(jnp.stack([gate_grad, up_grad]))], [gate_weight, up_weight], [gate_mask, up_mask], plan, (F32,), False
    )
    normed_grad = owner_sum(normed_grad)
    (grad_down,) = outer(hidden[0], seen_cot[None], [down_groups])
    grad_gate, grad_up = outer(seen_rows, grads, [gate_groups, up_groups])
    grad_tokens, grad_gain = finish(
        token_f,
        inv_rms,
        norm_gain,
        normed_grad,
        lambda value: lax.psum(value, "row"),
        lambda value: lax.psum(value, owners),
    )
    return (branch, grad_tokens, grad_gain, grad_gate, grad_up, grad_down)


def solution(mesh):
    split = P(("dp", "col"), "row")
    turned = P("row", ("dp", "col"))
    sizes = (mesh.shape["dp"], mesh.shape["row"], mesh.shape["col"])
    on_device = exchange_device if sizes == (2, 4, 4) else general_device
    return jax.shard_map(
        on_device,
        mesh=mesh,
        in_specs=(split, P("row"), turned, turned, split, turned, turned, split, split),
        out_specs=(split, split, P("row"), turned, turned, split),
        check_vma=False,
    )
```

```python
import functools
import jax
import jax.numpy as jnp
from jax import lax
from jax.experimental import pallas as pl
from jax.experimental.pallas import tpu as pltpu
from jax.sharding import PartitionSpec as P

BLOCK = 128
VMEM_BYTES = 10 * 1024 * 1024
BF16 = jnp.bfloat16
F32 = jnp.float32


def block_edge(extent):
    return 256 if extent % 256 == 0 else 128


def masked(weight, mask):
    groups, width = mask.shape
    shaped = weight.reshape(groups, BLOCK, width) * mask[:, None, :]
    return shaped.reshape(groups * BLOCK, width)


def swap(value, axis, size, step):
    return lax.ppermute(value, axis, [(i, i ^ step) for i in range(size)])


def kernel_params(steps=0):
    return pltpu.CompilerParams(
        dimension_semantics=("arbitrary",) * steps if steps else None, vmem_limit_bytes=VMEM_BYTES
    )


IN_VMEM = pl.BlockSpec(memory_space=pltpu.VMEM)
IN_SMEM = pl.BlockSpec(memory_space=pltpu.SMEM)


def place_rows(result, plan, outs, lead, columns):
    for ref, pieces in zip(outs, plan):
        at = 0
        for start, count in pieces:
            rows = result[start : start + count].astype(ref.dtype)
            if lead is None:
                ref[at : at + count, columns] = rows
            else:
                ref[lead, at : at + count, columns] = rows
            at += count


def plan_rows(pieces):
    return sum(count for _, count in pieces)


def bring_kernel(place_ref, *refs):
    refs[-1][0] = place_ref[0]


def bring(place, weights):
    return pl.pallas_call(
        bring_kernel,
        in_specs=[IN_SMEM] + [IN_VMEM] * len(weights),
        out_specs=IN_SMEM,
        out_shape=jax.ShapeDtypeStruct((1,), jnp.int32),
        compiler_params=kernel_params(),
        cost_estimate=pl.CostEstimate(flops=0, bytes_accessed=0, transcendentals=0),
    )(place, *weights)


def project_kernel(ring, plan, by_unit, amount, place_ref, *refs):
    parts, refs = refs[: max(1, 2 * ring)], refs[max(1, 2 * ring) :]
    weights, masks, rows_ref, outs = refs[:amount], refs[amount : 2 * amount], refs[2 * amount], refs[2 * amount + 1 :]
    if not ring:
        rows_ref[...] = parts[0][...]
    else:
        place = place_ref[0]
        unit = parts[0].shape[0]
        for slot in range(ring):
            for source in range(ring):

                @pl.when((place ^ slot) == source)
                def _(slot=slot, source=source):
                    at = 2 * unit * slot
                    rows_ref[at : at + unit, :] = parts[source][...]
                    rows_ref[at + unit : at + 2 * unit, :] = parts[ring + source][...]

    rows = rows_ref[...]
    units = weights[0].shape[0] if by_unit else weights[0].shape[1]
    edge = block_edge(units)
    for lead, (weight, mask) in enumerate(zip(weights, masks)):
        for at in range(0, units, edge):
            columns = slice(at, at + edge)
            if by_unit:
                kept = masked(weight[columns, :], mask[at // BLOCK : (at + edge) // BLOCK, :])
                result = lax.dot_general(rows, kept, (((1,), (1,)), ((), ())), preferred_element_type=F32)
            else:
                kept = masked(weight[:, columns], mask[:, columns])
                result = jnp.dot(rows, kept, preferred_element_type=F32)
            place_rows(result, plan, outs, lead, columns)


def project(place, parts, weights, masks, plan, by_unit, weigh=0):
    ring = len(parts) // 2
    amount = len(weights)
    features = parts[0].shape[1]
    tokens = sum(part.shape[0] for part in parts)
    units = weights[0].shape[0] if by_unit else weights[0].shape[1]
    counts = [plan_rows(pieces) for pieces in plan]
    return pl.pallas_call(
        functools.partial(project_kernel, ring, plan, by_unit, amount),
        in_specs=[IN_SMEM] + [IN_VMEM] * (len(parts) + 2 * amount),
        out_specs=[IN_VMEM] * (1 + len(plan)),
        out_shape=[jax.ShapeDtypeStruct((tokens, features), BF16)]
        + [jax.ShapeDtypeStruct((amount, count, units), BF16) for count in counts],
        compiler_params=kernel_params(),
        cost_estimate=pl.CostEstimate(
            flops=2 * tokens * features * units * amount * weigh,
            bytes_accessed=2 * amount * features * units * weigh,
            transcendentals=0,
        ),
    )(place, *parts, *weights, *masks)


def contract_kernel(pieces, plan, by_unit, amount, *refs):
    parts, refs = refs[: len(pieces)], refs[len(pieces) :]
    weights, masks, rows_ref, outs = refs[:amount], refs[amount : 2 * amount], refs[2 * amount], refs[2 * amount + 1 :]
    at = 0
    for part, count in zip(parts, pieces):
        rows_ref[:, at : at + count, :] = part[...]
        at += count
    rows = [rows_ref[lead] for lead in range(amount)]
    features = weights[0].shape[1] if by_unit else weights[0].shape[0]
    edge = block_edge(features)
    for at in range(0, features, edge):
        columns = slice(at, at + edge)
        total = None
        for lead, (weight, mask) in enumerate(zip(weights, masks)):
            if by_unit:
                kept = masked(weight[:, columns], mask[:, columns])
                result = jnp.dot(rows[lead], kept, preferred_element_type=F32)
            else:
                kept = masked(weight[columns, :], mask[at // BLOCK : (at + edge) // BLOCK, :])
                result = lax.dot_general(rows[lead], kept, (((1,), (1,)), ((), ())), preferred_element_type=F32)
            total = result if total is None else total + result
        place_rows(total, plan, outs, None, columns)


def contract(parts, weights, masks, plan, types, by_unit, weigh=0):
    amount = len(weights)
    units = parts[0].shape[2]
    pieces = [part.shape[1] for part in parts]
    tokens = sum(pieces)
    features = weights[0].shape[1] if by_unit else weights[0].shape[0]
    counts = [plan_rows(piece) for piece in plan]
    return pl.pallas_call(
        functools.partial(contract_kernel, pieces, plan, by_unit, amount),
        in_specs=[IN_VMEM] * (len(parts) + 2 * amount),
        out_specs=[IN_VMEM] * (1 + len(plan)),
        out_shape=[jax.ShapeDtypeStruct((amount, tokens, units), BF16)]
        + [jax.ShapeDtypeStruct((count, features), kind) for count, kind in zip(counts, types)],
        compiler_params=kernel_params(),
        cost_estimate=pl.CostEstimate(
            flops=2 * tokens * features * units * amount * weigh,
            bytes_accessed=2 * amount * features * units * weigh,
            transcendentals=0,
        ),
    )(*parts, *weights, *masks)


def outer_kernel(left_ref, right_ref, *refs):
    amount = right_ref.shape[0]
    masks, outs = refs[:amount], refs[amount:]
    edge = outs[0].shape[0]
    left = left_ref[:, pl.ds(pl.multiple_of(pl.program_id(0) * edge, edge), edge)]
    for lead in range(amount):
        result = lax.dot_general(left, right_ref[lead], (((0,), (0,)), ((), ())), preferred_element_type=F32)
        outs[lead][...] = masked(result, masks[lead][0].astype(F32))


def outer(left, right, masks):
    tokens, rows = left.shape
    amount, _, width = right.shape
    edge = block_edge(rows)
    return pl.pallas_call(
        outer_kernel,
        grid=(rows // edge,),
        in_specs=[IN_VMEM, IN_VMEM] + [pl.BlockSpec((1, edge // BLOCK, width), lambda j: (j, 0, 0))] * amount,
        out_specs=[pl.BlockSpec((edge, width), lambda j: (j, 0))] * amount,
        out_shape=[jax.ShapeDtypeStruct((rows, width), F32)] * amount,
        compiler_params=kernel_params(1),
        cost_estimate=pl.CostEstimate(
            flops=0, bytes_accessed=0, transcendentals=0
        ),
    )(left, right, *masks)


def owner_kernel(count, place_ref, own_ref, got_ref, *refs):
    factors = refs[:count] if len(refs) > count else ()
    outs = refs[len(factors) : len(factors) + count]
    unit = outs[0].shape[0]
    place = place_ref[0]
    down = None
    for step in range(count):
        rows = pl.ds(pl.multiple_of((place ^ step) * unit, 16), unit)
        part = own_ref[rows, :] + got_ref[rows, :].astype(F32)
        outs[step][...] = part.astype(outs[step].dtype)
        if factors:
            step_down = jnp.sum(part * factors[step][...].astype(F32), axis=0, keepdims=True)
            down = step_down if down is None else down + step_down
    if factors:
        refs[-1][...] = down


def owner(place, own, got, count, factors=()):
    total, features = own.shape
    unit = total // count
    outs = [jax.ShapeDtypeStruct((unit, features), F32 if step == 0 else BF16) for step in range(count)]
    if factors:
        outs += [jax.ShapeDtypeStruct((1, features), F32)]
    return pl.pallas_call(
        functools.partial(owner_kernel, count),
        in_specs=[IN_SMEM] + [IN_VMEM] * (2 + len(factors)),
        out_specs=[IN_VMEM] * len(outs),
        out_shape=outs,
        compiler_params=kernel_params(),
    )(place, own, got, *factors)


def activation(gate, up_value, hidden_grad):
    sigmoid_gate = 1.0 / (1.0 + jnp.exp(-gate))
    scaled = gate * sigmoid_gate
    hidden = scaled * up_value
    gate_grad = hidden_grad * up_value * sigmoid_gate * (1.0 + gate * (1.0 - sigmoid_gate))
    up_grad = hidden_grad * scaled
    return hidden, gate_grad, up_grad


def activate_kernel(*refs):
    gates, ups, ones, (hidden_ref, grads_ref, sums_ref, held_ref) = refs[:5], refs[5:10], refs[10:15], refs[15:]
    half = gates[3].shape[1]
    for second in (False, True):
        at = half if second else 0
        rows = slice(at, at + half)

        def summed(parts):
            own, first_x, first_y, last_y, last_x = parts
            first, last = (first_y, last_x) if second else (first_x, last_y)
            return own[0, rows].astype(F32) + first[0, half:].astype(F32) + last[0].astype(F32)

        gate, up_value = summed(gates), summed(ups)
        hidden, *grads = activation(gate, up_value, summed(ones))
        hidden_ref[0, rows] = hidden.astype(BF16)
        products = 0.0
        for lead, (grad, value) in enumerate(zip(grads, (gate, up_value))):
            rounded = grad.astype(BF16)
            grads_ref[lead, rows] = rounded
            products = products + rounded.astype(F32) * value

        @pl.when(pl.program_id(0) == 0)
        def _():
            held_ref[rows] = products

        @pl.when(pl.program_id(0) > 0)
        def _():
            held_ref[rows] = held_ref[rows] + products

    @pl.when(pl.program_id(0) == pl.num_programs(0) - 1)
    def _():
        sums_ref[...] = jnp.broadcast_to(jnp.sum(held_ref[...], axis=1, keepdims=True), sums_ref.shape)


def activate(gates, ups, ones):
    _, share, units = gates[0].shape
    edge = block_edge(units)
    spec = lambda array: pl.BlockSpec(array.shape[:2] + (edge,), lambda j: (0, 0, j))
    outs = [jax.ShapeDtypeStruct((amount, share, units), BF16) for amount in (1, 2)]
    return pl.pallas_call(
        activate_kernel,
        grid=(units // edge,),
        in_specs=[spec(array) for array in gates + ups + ones],
        out_specs=[spec(array) for array in outs] + [pl.BlockSpec((share, BLOCK), lambda j: (0, 0))],
        out_shape=outs + [jax.ShapeDtypeStruct((share, BLOCK), F32)],
        scratch_shapes=[pltpu.VMEM((share, edge), F32)],
        compiler_params=kernel_params(1),
    )(*gates, *ups, *ones)


def widen(keep):
    return jnp.repeat(keep, BLOCK, axis=1).astype(BF16)


def widen_grouped(keep):
    together = block_edge(keep.shape[0] * BLOCK) // BLOCK
    return widen(keep).reshape(-1, together, keep.shape[1] * BLOCK)


def finish(token_f, inv_rms, norm_gain, normed_grad, inner_sum, gain_sum):
    grad_gain = gain_sum(jnp.sum(normed_grad * token_f * inv_rms, axis=0))
    inner_dot = inner_sum(jnp.sum(norm_gain * normed_grad * token_f, axis=1))
    width = norm_gain.shape[0] * lax.axis_size("row")
    grad_tokens = (
        inv_rms * norm_gain * normed_grad
        - token_f * inv_rms * inv_rms * inv_rms * inner_dot[:, None] / width
    )
    return grad_tokens, grad_gain


def ordered(*groups):
    return lax.optimization_barrier(groups)


def exchange_device(
    tokens, norm_gain, gate_weight, up_weight, down_weight, gate_keep, up_keep, down_keep, cotangent
):
    rows, cols = 4, 4
    unit, features = tokens.shape
    place = lax.axis_index("row")
    place_arg = place.astype(jnp.int32).reshape(1)

    def core_swap(value):
        return swap(value, "dp", 2, 1)

    def row_swap(value, step):
        return swap(value, "row", rows, step)

    def level_swaps(parts):
        return [swap(part, "col", cols, step + 1) for step, part in enumerate(parts)]

    def balanced(value, got):
        return (value + got[0]) + (got[1] + got[2])

    def row_sum(value):
        value = value + row_swap(value, 1)
        return value + row_swap(value, 2)

    def sum_first(x_first, y_first):
        return ordered(row_swap(x_first, 1), row_swap(y_first, 2))

    def sum_middle(x_keep, y_keep, got_x, got_y):
        half = x_keep.shape[1]
        add = lambda a, b: (a.astype(F32) + b[:, :half].astype(F32)).astype(BF16)
        return add(y_keep, got_x), add(x_keep, got_y)

    def sum_last(for_y, for_x):
        return ordered(row_swap(for_y, 2), row_swap(for_x, 1))

    def gather_first(share):
        return ordered(row_swap(share, 1), row_swap(share, 2))

    def gather_middle(got_x, got_y):
        return got_y[:, :unit], got_x[:, unit:]

    def gather_last(for_x, for_y):
        return ordered(row_swap(for_x, 1), row_swap(for_y, 2))

    def owner_total(kept, got):
        return balanced(kept, [part.astype(F32) for part in got])

    def rows_of(slot, second):
        return (2 * unit * slot + (unit if second else 0), unit)

    first_plan = [
        [rows_of(3, False), rows_of(1, False)],
        [rows_of(3, True), rows_of(2, True)],
        [rows_of(1, True)],
        [rows_of(2, False)],
        [(0, 2 * unit)],
    ]
    last_plan = [[rows_of(slot, False) for slot in range(rows)], [rows_of(slot, True) for slot in range(rows)]]

    token_f = tokens.astype(F32)
    squares = jnp.sum(token_f * token_f, axis=1)
    cot_far = level_swaps([cotangent] * 3)
    inv_rms = lax.rsqrt(row_sum(squares)[:, None] / (features * rows) + 1e-05)
    normed = (token_f * inv_rms * norm_gain).astype(BF16)
    gate_mask, up_mask, down_mask = widen(gate_keep), widen(up_keep), widen(down_keep)
    gate_groups, up_groups, down_groups = widen_grouped(gate_keep), widen_grouped(up_keep), widen_grouped(down_keep)
    cot_core, normed_core = core_swap(cotangent), core_swap(normed)
    masks = [gate_mask, up_mask, down_mask, gate_groups, up_groups, down_groups]
    place, place_arg, masks = ordered(place, place_arg, masks)
    gate_mask, up_mask, down_mask, gate_groups, up_groups, down_groups = masks
    place_arg = bring(place_arg, [down_weight, gate_weight, up_weight])
    cot_far, cot_core, normed, normed_core, place_arg = ordered(cot_far, cot_core, normed, normed_core, place_arg)
    cot_own = [cotangent, *cot_far]
    cot_other = [cot_core] + [core_swap(part) for part in cot_far]

    normed_far = level_swaps([normed] * 3)
    seen_cot, *one_parts = project(
        place_arg, cot_own + cot_other, [down_weight], [down_mask], first_plan, True
    )
    one_x, one_y = sum_first(*one_parts[:2])
    normed_far, one_keep = ordered(normed_far, one_parts[2:])
    normed_own = [normed, *normed_far]
    normed_other = [normed_core] + [core_swap(part) for part in normed_far]

    seen_rows, *gate_parts = project(
        place_arg, normed_own + normed_other, [gate_weight], [gate_mask], first_plan, False
    )
    gate_x, gate_y = sum_first(*gate_parts[:2])
    _, *up_parts = project(place_arg, [seen_rows], [up_weight], [up_mask], first_plan, False)
    one_x, one_y, up_parts = ordered(one_x, one_y, up_parts)
    up_x, up_y = sum_first(*up_parts[:2])
    one_middle = sum_middle(*one_keep[:2], one_x, one_y)
    gate_x, gate_y, up_parts, one_middle = ordered(gate_x, gate_y, up_parts, one_middle)
    gate_last = sum_last(*sum_middle(*gate_parts[2:4], gate_x, gate_y))
    up_x, up_y, one_middle = ordered(up_x, up_y, one_middle)
    one_last = sum_last(*one_middle)
    up_last = sum_last(*sum_middle(*up_parts[2:4], up_x, up_y))
    hidden_share, grads_share, inner_share = activate(
        [gate_parts[4], gate_x, gate_y, *gate_last],
        [up_parts[4], up_x, up_y, *up_last],
        [one_keep[2], one_x, one_y, *one_last],
    )

    hidden_x, hidden_y = gather_first(hidden_share)
    hidden_middle = gather_middle(hidden_x, hidden_y)
    grads_share, hidden_middle = ordered(grads_share, hidden_middle)
    grads_x, grads_y = gather_first(grads_share)
    hidden_last = gather_last(*hidden_middle)
    hidden, branch_own, branch_other = contract(
        [hidden_share, hidden_x, hidden_y, *hidden_last], [down_weight], [down_mask], last_plan, (F32, BF16), True, 10
    )
    inner_share, branch_own = ordered(inner_share, branch_own)
    inner = inner_share[:unit] + core_swap(inner_share[unit:])
    to_owner = [(r * cols + z, r * cols + (z ^ r)) for r in range(rows) for z in range(cols)]
    inner = lax.ppermute(inner, ("row", "col"), to_owner)
    grads_x, grads_y, branch_own, branch_other, inner = ordered(grads_x, grads_y, branch_own, branch_other, inner)
    branch_got = core_swap(branch_other)
    grads_middle = gather_middle(grads_x, grads_y)
    grads_last = gather_last(*grads_middle)
    branch_kept, *branch_parts = owner(place_arg, branch_own, branch_got, cols)
    branch_far = level_swaps(branch_parts)
    hidden, grads_middle = ordered(hidden, grads_middle)
    (grad_down,) = outer(hidden[0], seen_cot[None], [down_groups])
    grads_last, grad_down = ordered(grads_last, grad_down)

    grads, normed_mine, normed_theirs = contract(
        [grads_share, grads_x, grads_y, *grads_last], [gate_weight, up_weight], [gate_mask, up_mask], last_plan, (F32, BF16), False
    )
    branch_far, normed_mine, normed_theirs = ordered(branch_far, normed_mine, normed_theirs)

    kept, *parts, down_sum = owner(place_arg, normed_mine, core_swap(normed_theirs), cols, normed_own)
    grads, parts, down_sum, inner = ordered(grads, parts, down_sum, inner)
    far = level_swaps(parts)
    down_pair = down_sum + swap(down_sum, "col", cols, 1)
    inner_pair = inner + row_swap(inner, 1)
    grads, down_pair, inner_pair = ordered(grads, down_pair, inner_pair)
    down_got = swap(down_pair, "col", cols, 2)
    inner_got = row_swap(inner_pair, 2)
    grad_gate, grad_up = outer(seen_rows, grads, [gate_groups, up_groups])
    far, down_got, inner_got, grad_gate, grad_up = ordered(far, down_got, inner_got, grad_gate, grad_up)
    inner = inner_pair + inner_got
    down_levels = down_pair + down_got
    down_total = down_levels + core_swap(down_levels)
    branch = owner_total(branch_kept, branch_far).astype(BF16)
    normed_grad = owner_total(kept, far)
    grad_gain = down_total.reshape(features) / norm_gain
    grad_tokens = (
        inv_rms * norm_gain * normed_grad - token_f * inv_rms * inv_rms * inner[:, :1] / (features * rows)
    )
    return (branch, grad_tokens, grad_gain, grad_gate, grad_up, grad_down)


def general_device(
    tokens, norm_gain, gate_weight, up_weight, down_weight, gate_keep, up_keep, down_keep, cotangent
):
    owners = ("dp", "col")
    features = tokens.shape[1]
    place_arg = jnp.zeros((1,), jnp.int32)
    token_f = tokens.astype(F32)
    square = lax.psum(jnp.sum(token_f * token_f, axis=1), "row")
    inv_rms = lax.rsqrt(square[:, None] / (features * lax.axis_size("row")) + 1e-05)
    normed = (token_f * inv_rms * norm_gain).astype(BF16)
    gate_mask, up_mask, down_mask = widen(gate_keep), widen(up_keep), widen(down_keep)
    gate_groups, up_groups, down_groups = widen_grouped(gate_keep), widen_grouped(up_keep), widen_grouped(down_keep)
    seen_cot = lax.all_gather(cotangent, owners, axis=0, tiled=True)
    seen_rows = lax.all_gather(normed, owners, axis=0, tiled=True)
    plan = [[(0, seen_cot.shape[0])]]

    def share(value):
        return lax.psum_scatter(value.astype(F32), "row", scatter_dimension=1, tiled=True)

    def collect(value):
        return lax.all_gather(value.astype(BF16), "row", axis=1, tiled=True)

    def owner_sum(value):
        return lax.psum_scatter(value, owners, scatter_dimension=0, tiled=True)

    _, one = project(place_arg, [seen_cot], [down_weight], [down_mask], plan, True)
    _, pair = project(place_arg, [seen_rows], [gate_weight, up_weight], [gate_mask, up_mask], plan, False)
    pair = share(pair)
    hidden, gate_grad, up_grad = activation(pair[0], pair[1], share(one)[0])
    hidden, branch = contract([collect(hidden[None])], [down_weight], [down_mask], plan, (F32,), True)
    branch = owner_sum(branch).astype(BF16)
    grads, normed_grad = contract(
        [collect(jnp.stack([gate_grad, up_grad]))], [gate_weight, up_weight], [gate_mask, up_mask], plan, (F32,), False
    )
    normed_grad = owner_sum(normed_grad)
    (grad_down,) = outer(hidden[0], seen_cot[None], [down_groups])
    grad_gate, grad_up = outer(seen_rows, grads, [gate_groups, up_groups])
    grad_tokens, grad_gain = finish(
        token_f,
        inv_rms,
        norm_gain,
        normed_grad,
        lambda value: lax.psum(value, "row"),
        lambda value: lax.psum(value, owners),
    )
    return (branch, grad_tokens, grad_gain, grad_gate, grad_up, grad_down)


def solution(mesh):
    split = P(("dp", "col"), "row")
    turned = P("row", ("dp", "col"))
    sizes = (mesh.shape["dp"], mesh.shape["row"], mesh.shape["col"])
    on_device = exchange_device if sizes == (2, 4, 4) else general_device
    return jax.shard_map(
        on_device,
        mesh=mesh,
        in_specs=(split, P("row"), turned, turned, split, turned, turned, split, split),
        out_specs=(split, split, P("row"), turned, turned, split),
        check_vma=False,
    )
```

```python
import functools
import jax
import jax.numpy as jnp
from jax import lax
from jax.experimental import pallas as pl
from jax.experimental.pallas import tpu as pltpu
from jax.sharding import PartitionSpec as P

BLOCK = 128
VMEM_BYTES = 10 * 1024 * 1024
BF16 = jnp.bfloat16
F32 = jnp.float32


def block_edge(extent):
    return 256 if extent % 256 == 0 else 128


def masked(weight, mask):
    groups, width = mask.shape
    shaped = weight.reshape(groups, BLOCK, width) * mask[:, None, :]
    return shaped.reshape(groups * BLOCK, width)


def swap(value, axis, size, step):
    return lax.ppermute(value, axis, [(i, i ^ step) for i in range(size)])


def kernel_params(steps=0):
    return pltpu.CompilerParams(
        dimension_semantics=("arbitrary",) * steps if steps else None, vmem_limit_bytes=VMEM_BYTES
    )


IN_VMEM = pl.BlockSpec(memory_space=pltpu.VMEM)
IN_SMEM = pl.BlockSpec(memory_space=pltpu.SMEM)


def place_rows(result, plan, outs, lead, columns):
    for ref, pieces in zip(outs, plan):
        at = 0
        for start, count in pieces:
            rows = result[start : start + count].astype(ref.dtype)
            if lead is None:
                ref[at : at + count, columns] = rows
            else:
                ref[lead, at : at + count, columns] = rows
            at += count


def plan_rows(pieces):
    return sum(count for _, count in pieces)


def bring_kernel(place_ref, *refs):
    refs[-1][0] = place_ref[0]


def bring(place, weights):
    return pl.pallas_call(
        bring_kernel,
        in_specs=[IN_SMEM] + [IN_VMEM] * len(weights),
        out_specs=IN_SMEM,
        out_shape=jax.ShapeDtypeStruct((1,), jnp.int32),
        compiler_params=kernel_params(),
        cost_estimate=pl.CostEstimate(flops=0, bytes_accessed=0, transcendentals=0),
    )(place, *weights)


def project_kernel(ring, plan, by_unit, amount, place_ref, *refs):
    parts, refs = refs[: max(1, 2 * ring)], refs[max(1, 2 * ring) :]
    weights, masks, rows_ref, outs = refs[:amount], refs[amount : 2 * amount], refs[2 * amount], refs[2 * amount + 1 :]
    if not ring:
        rows_ref[...] = parts[0][...]
    else:
        place = place_ref[0]
        unit = parts[0].shape[0]
        for slot in range(ring):
            for source in range(ring):

                @pl.when((place ^ slot) == source)
                def _(slot=slot, source=source):
                    at = 2 * unit * slot
                    rows_ref[at : at + unit, :] = parts[source][...]
                    rows_ref[at + unit : at + 2 * unit, :] = parts[ring + source][...]

    rows = rows_ref[...]
    units = weights[0].shape[0] if by_unit else weights[0].shape[1]
    edge = block_edge(units)
    for lead, (weight, mask) in enumerate(zip(weights, masks)):
        for at in range(0, units, edge):
            columns = slice(at, at + edge)
            if by_unit:
                kept = masked(weight[columns, :], mask[at // BLOCK : (at + edge) // BLOCK, :])
                result = lax.dot_general(rows, kept, (((1,), (1,)), ((), ())), preferred_element_type=F32)
            else:
                kept = masked(weight[:, columns], mask[:, columns])
                result = jnp.dot(rows, kept, preferred_element_type=F32)
            place_rows(result, plan, outs, lead, columns)


def project(place, parts, weights, masks, plan, by_unit, weigh=0):
    ring = len(parts) // 2
    amount = len(weights)
    features = parts[0].shape[1]
    tokens = sum(part.shape[0] for part in parts)
    units = weights[0].shape[0] if by_unit else weights[0].shape[1]
    counts = [plan_rows(pieces) for pieces in plan]
    return pl.pallas_call(
        functools.partial(project_kernel, ring, plan, by_unit, amount),
        in_specs=[IN_SMEM] + [IN_VMEM] * (len(parts) + 2 * amount),
        out_specs=[IN_VMEM] * (1 + len(plan)),
        out_shape=[jax.ShapeDtypeStruct((tokens, features), BF16)]
        + [jax.ShapeDtypeStruct((amount, count, units), BF16) for count in counts],
        compiler_params=kernel_params(),
        cost_estimate=pl.CostEstimate(
            flops=2 * tokens * features * units * amount * weigh,
            bytes_accessed=2 * amount * features * units * weigh,
            transcendentals=0,
        ),
    )(place, *parts, *weights, *masks)


def contract_kernel(pieces, plan, by_unit, amount, *refs):
    parts, refs = refs[: len(pieces)], refs[len(pieces) :]
    weights, masks, rows_ref, outs = refs[:amount], refs[amount : 2 * amount], refs[2 * amount], refs[2 * amount + 1 :]
    at = 0
    for part, count in zip(parts, pieces):
        rows_ref[:, at : at + count, :] = part[...]
        at += count
    rows = [rows_ref[lead] for lead in range(amount)]
    features = weights[0].shape[1] if by_unit else weights[0].shape[0]
    edge = block_edge(features)
    for at in range(0, features, edge):
        columns = slice(at, at + edge)
        total = None
        for lead, (weight, mask) in enumerate(zip(weights, masks)):
            if by_unit:
                kept = masked(weight[:, columns], mask[:, columns])
                result = jnp.dot(rows[lead], kept, preferred_element_type=F32)
            else:
                kept = masked(weight[columns, :], mask[at // BLOCK : (at + edge) // BLOCK, :])
                result = lax.dot_general(rows[lead], kept, (((1,), (1,)), ((), ())), preferred_element_type=F32)
            total = result if total is None else total + result
        place_rows(total, plan, outs, None, columns)


def contract(parts, weights, masks, plan, types, by_unit, weigh=0):
    amount = len(weights)
    units = parts[0].shape[2]
    pieces = [part.shape[1] for part in parts]
    tokens = sum(pieces)
    features = weights[0].shape[1] if by_unit else weights[0].shape[0]
    counts = [plan_rows(piece) for piece in plan]
    return pl.pallas_call(
        functools.partial(contract_kernel, pieces, plan, by_unit, amount),
        in_specs=[IN_VMEM] * (len(parts) + 2 * amount),
        out_specs=[IN_VMEM] * (1 + len(plan)),
        out_shape=[jax.ShapeDtypeStruct((amount, tokens, units), BF16)]
        + [jax.ShapeDtypeStruct((count, features), kind) for count, kind in zip(counts, types)],
        compiler_params=kernel_params(),
        cost_estimate=pl.CostEstimate(
            flops=2 * tokens * features * units * amount * weigh,
            bytes_accessed=2 * amount * features * units * weigh,
            transcendentals=0,
        ),
    )(*parts, *weights, *masks)


def outer_kernel(left_ref, right_ref, *refs):
    amount = right_ref.shape[0]
    masks, outs = refs[:amount], refs[amount:]
    edge = outs[0].shape[0]
    left = left_ref[:, pl.ds(pl.multiple_of(pl.program_id(0) * edge, edge), edge)]
    for lead in range(amount):
        result = lax.dot_general(left, right_ref[lead], (((0,), (0,)), ((), ())), preferred_element_type=F32)
        outs[lead][...] = masked(result, masks[lead][0].astype(F32))


def outer(left, right, masks):
    tokens, rows = left.shape
    amount, _, width = right.shape
    edge = block_edge(rows)
    return pl.pallas_call(
        outer_kernel,
        grid=(rows // edge,),
        in_specs=[IN_VMEM, IN_VMEM] + [pl.BlockSpec((1, edge // BLOCK, width), lambda j: (j, 0, 0))] * amount,
        out_specs=[pl.BlockSpec((edge, width), lambda j: (j, 0))] * amount,
        out_shape=[jax.ShapeDtypeStruct((rows, width), F32)] * amount,
        compiler_params=kernel_params(1),
        cost_estimate=pl.CostEstimate(
            flops=0, bytes_accessed=0, transcendentals=0
        ),
    )(left, right, *masks)


def outer_one_kernel(left_ref, right_ref, mask_ref, out_ref, held_ref, sems):
    slots, edge, _ = held_ref.shape
    copies = []
    for block in range(left_ref.shape[1] // edge):
        rows = slice(block * edge, (block + 1) * edge)
        slot = block % slots
        if block >= slots:
            copies[block - slots].wait()
        result = lax.dot_general(
            left_ref[:, rows], right_ref[...], (((0,), (0,)), ((), ())), preferred_element_type=F32
        )
        held_ref[slot] = masked(result, mask_ref[block].astype(F32))
        copies.append(pltpu.make_async_copy(held_ref.at[slot], out_ref.at[rows], sems.at[slot]))
        copies[-1].start()
    for copy in copies[-slots:]:
        copy.wait()


def outer_one(left, right, mask):
    rows, width = left.shape[1], right.shape[1]
    edge = block_edge(rows)
    return pl.pallas_call(
        outer_one_kernel,
        in_specs=[IN_VMEM] * 3,
        out_specs=pl.BlockSpec(memory_space=pl.ANY),
        out_shape=jax.ShapeDtypeStruct((rows, width), F32),
        scratch_shapes=[pltpu.VMEM((3, edge, width), F32), pltpu.SemaphoreType.DMA((3,))],
        compiler_params=kernel_params(),
        cost_estimate=pl.CostEstimate(flops=0, bytes_accessed=0, transcendentals=0),
    )(left, right, mask)


def owner_kernel(count, place_ref, own_ref, got_ref, *refs):
    factors = refs[:count] if len(refs) > count else ()
    outs = refs[len(factors) : len(factors) + count]
    unit = outs[0].shape[0]
    place = place_ref[0]
    down = None
    for step in range(count):
        rows = pl.ds(pl.multiple_of((place ^ step) * unit, 16), unit)
        part = own_ref[rows, :] + got_ref[rows, :].astype(F32)
        outs[step][...] = part.astype(outs[step].dtype)
        if factors:
            step_down = jnp.sum(part * factors[step][...].astype(F32), axis=0, keepdims=True)
            down = step_down if down is None else down + step_down
    if factors:
        refs[-1][...] = down


def owner(place, own, got, count, factors=()):
    total, features = own.shape
    unit = total // count
    outs = [jax.ShapeDtypeStruct((unit, features), F32 if step == 0 else BF16) for step in range(count)]
    if factors:
        outs += [jax.ShapeDtypeStruct((1, features), F32)]
    return pl.pallas_call(
        functools.partial(owner_kernel, count),
        in_specs=[IN_SMEM] + [IN_VMEM] * (2 + len(factors)),
        out_specs=[IN_VMEM] * len(outs),
        out_shape=outs,
        compiler_params=kernel_params(),
    )(place, own, got, *factors)


def activation(gate, up_value, hidden_grad):
    sigmoid_gate = 1.0 / (1.0 + jnp.exp(-gate))
    scaled = gate * sigmoid_gate
    hidden = scaled * up_value
    gate_grad = hidden_grad * up_value * sigmoid_gate * (1.0 + gate * (1.0 - sigmoid_gate))
    up_grad = hidden_grad * scaled
    return hidden, gate_grad, up_grad


def activate_kernel(*refs):
    gates, ups, ones, (hidden_ref, grads_ref, sums_ref, held_ref) = refs[:5], refs[5:10], refs[10:15], refs[15:]
    half = gates[3].shape[1]
    for second in (False, True):
        at = half if second else 0
        rows = slice(at, at + half)

        def summed(parts):
            own, first_x, first_y, last_y, last_x = parts
            first, last = (first_y, last_x) if second else (first_x, last_y)
            return own[0, rows].astype(F32) + first[0, half:].astype(F32) + last[0].astype(F32)

        gate, up_value = summed(gates), summed(ups)
        hidden, *grads = activation(gate, up_value, summed(ones))
        hidden_ref[0, rows] = hidden.astype(BF16)
        products = 0.0
        for lead, (grad, value) in enumerate(zip(grads, (gate, up_value))):
            rounded = grad.astype(BF16)
            grads_ref[lead, rows] = rounded
            products = products + rounded.astype(F32) * value

        @pl.when(pl.program_id(0) == 0)
        def _():
            held_ref[rows] = products

        @pl.when(pl.program_id(0) > 0)
        def _():
            held_ref[rows] = held_ref[rows] + products

    @pl.when(pl.program_id(0) == pl.num_programs(0) - 1)
    def _():
        sums_ref[...] = jnp.broadcast_to(jnp.sum(held_ref[...], axis=1, keepdims=True), sums_ref.shape)


def activate(gates, ups, ones):
    _, share, units = gates[0].shape
    edge = block_edge(units)
    spec = lambda array: pl.BlockSpec(array.shape[:2] + (edge,), lambda j: (0, 0, j))
    outs = [jax.ShapeDtypeStruct((amount, share, units), BF16) for amount in (1, 2)]
    return pl.pallas_call(
        activate_kernel,
        grid=(units // edge,),
        in_specs=[spec(array) for array in gates + ups + ones],
        out_specs=[spec(array) for array in outs] + [pl.BlockSpec((share, BLOCK), lambda j: (0, 0))],
        out_shape=outs + [jax.ShapeDtypeStruct((share, BLOCK), F32)],
        scratch_shapes=[pltpu.VMEM((share, edge), F32)],
        compiler_params=kernel_params(1),
    )(*gates, *ups, *ones)


def widen(keep):
    return jnp.repeat(keep, BLOCK, axis=1).astype(BF16)


def widen_grouped(keep):
    together = block_edge(keep.shape[0] * BLOCK) // BLOCK
    return widen(keep).reshape(-1, together, keep.shape[1] * BLOCK)


def finish(token_f, inv_rms, norm_gain, normed_grad, inner_sum, gain_sum):
    grad_gain = gain_sum(jnp.sum(normed_grad * token_f * inv_rms, axis=0))
    inner_dot = inner_sum(jnp.sum(norm_gain * normed_grad * token_f, axis=1))
    width = norm_gain.shape[0] * lax.axis_size("row")
    grad_tokens = (
        inv_rms * norm_gain * normed_grad
        - token_f * inv_rms * inv_rms * inv_rms * inner_dot[:, None] / width
    )
    return grad_tokens, grad_gain


def ordered(*groups):
    return lax.optimization_barrier(groups)


def exchange_device(
    tokens, norm_gain, gate_weight, up_weight, down_weight, gate_keep, up_keep, down_keep, cotangent
):
    rows, cols = 4, 4
    unit, features = tokens.shape
    place = lax.axis_index("row")
    place_arg = place.astype(jnp.int32).reshape(1)

    def core_swap(value):
        return swap(value, "dp", 2, 1)

    def row_swap(value, step):
        return swap(value, "row", rows, step)

    def level_swaps(parts):
        return [swap(part, "col", cols, step + 1) for step, part in enumerate(parts)]

    def balanced(value, got):
        return (value + got[0]) + (got[1] + got[2])

    def row_sum(value):
        value = value + row_swap(value, 1)
        return value + row_swap(value, 2)

    def sum_first(x_first, y_first):
        return ordered(row_swap(x_first, 1), row_swap(y_first, 2))

    def sum_middle(x_keep, y_keep, got_x, got_y):
        half = x_keep.shape[1]
        add = lambda a, b: (a.astype(F32) + b[:, :half].astype(F32)).astype(BF16)
        return add(y_keep, got_x), add(x_keep, got_y)

    def sum_last(for_y, for_x):
        return ordered(row_swap(for_y, 2), row_swap(for_x, 1))

    def gather_first(share):
        return ordered(row_swap(share, 1), row_swap(share, 2))

    def gather_middle(got_x, got_y):
        return got_y[:, :unit], got_x[:, unit:]

    def gather_last(for_x, for_y):
        return ordered(row_swap(for_x, 1), row_swap(for_y, 2))

    def owner_total(kept, got):
        return balanced(kept, [part.astype(F32) for part in got])

    def rows_of(slot, second):
        return (2 * unit * slot + (unit if second else 0), unit)

    first_plan = [
        [rows_of(3, False), rows_of(1, False)],
        [rows_of(3, True), rows_of(2, True)],
        [rows_of(1, True)],
        [rows_of(2, False)],
        [(0, 2 * unit)],
    ]
    last_plan = [[rows_of(slot, False) for slot in range(rows)], [rows_of(slot, True) for slot in range(rows)]]

    token_f = tokens.astype(F32)
    squares = jnp.sum(token_f * token_f, axis=1)
    cot_far = level_swaps([cotangent] * 3)
    inv_rms = lax.rsqrt(row_sum(squares)[:, None] / (features * rows) + 1e-05)
    normed = (token_f * inv_rms * norm_gain).astype(BF16)
    gate_mask, up_mask, down_mask = widen(gate_keep), widen(up_keep), widen(down_keep)
    gate_groups, up_groups, down_groups = widen_grouped(gate_keep), widen_grouped(up_keep), widen_grouped(down_keep)
    cot_core, normed_core = core_swap(cotangent), core_swap(normed)
    masks = [gate_mask, up_mask, down_mask, gate_groups, up_groups, down_groups]
    place, place_arg, masks = ordered(place, place_arg, masks)
    gate_mask, up_mask, down_mask, gate_groups, up_groups, down_groups = masks
    place_arg = bring(place_arg, [down_weight, gate_weight, up_weight])
    cot_far, cot_core, normed, normed_core, place_arg = ordered(cot_far, cot_core, normed, normed_core, place_arg)
    cot_own = [cotangent, *cot_far]
    cot_other = [cot_core] + [core_swap(part) for part in cot_far]

    normed_far = level_swaps([normed] * 3)
    seen_cot, *one_parts = project(
        place_arg, cot_own + cot_other, [down_weight], [down_mask], first_plan, True
    )
    one_x, one_y = sum_first(*one_parts[:2])
    normed_far, one_keep = ordered(normed_far, one_parts[2:])
    normed_own = [normed, *normed_far]
    normed_other = [normed_core] + [core_swap(part) for part in normed_far]

    seen_rows, *gate_parts = project(
        place_arg, normed_own + normed_other, [gate_weight], [gate_mask], first_plan, False
    )
    gate_x, gate_y = sum_first(*gate_parts[:2])
    _, *up_parts = project(place_arg, [seen_rows], [up_weight], [up_mask], first_plan, False)
    one_x, one_y, up_parts = ordered(one_x, one_y, up_parts)
    up_x, up_y = sum_first(*up_parts[:2])
    one_middle = sum_middle(*one_keep[:2], one_x, one_y)
    gate_x, gate_y, up_parts, one_middle = ordered(gate_x, gate_y, up_parts, one_middle)
    gate_last = sum_last(*sum_middle(*gate_parts[2:4], gate_x, gate_y))
    up_x, up_y, one_middle = ordered(up_x, up_y, one_middle)
    one_last = sum_last(*one_middle)
    up_last = sum_last(*sum_middle(*up_parts[2:4], up_x, up_y))
    hidden_share, grads_share, inner_share = activate(
        [gate_parts[4], gate_x, gate_y, *gate_last],
        [up_parts[4], up_x, up_y, *up_last],
        [one_keep[2], one_x, one_y, *one_last],
    )

    hidden_x, hidden_y = gather_first(hidden_share)
    hidden_middle = gather_middle(hidden_x, hidden_y)
    grads_share, hidden_middle = ordered(grads_share, hidden_middle)
    grads_x, grads_y = gather_first(grads_share)
    hidden_last = gather_last(*hidden_middle)
    hidden, branch_own, branch_other = contract(
        [hidden_share, hidden_x, hidden_y, *hidden_last], [down_weight], [down_mask], last_plan, (F32, BF16), True, 10
    )
    inner_share, branch_own = ordered(inner_share, branch_own)
    inner = inner_share[:unit] + core_swap(inner_share[unit:])
    to_owner = [(r * cols + z, r * cols + (z ^ r)) for r in range(rows) for z in range(cols)]
    inner = lax.ppermute(inner, ("row", "col"), to_owner)
    grads_x, grads_y, branch_own, branch_other, inner = ordered(grads_x, grads_y, branch_own, branch_other, inner)
    branch_got = core_swap(branch_other)
    grads_middle = gather_middle(grads_x, grads_y)
    grads_last = gather_last(*grads_middle)
    branch_kept, *branch_parts = owner(place_arg, branch_own, branch_got, cols)
    branch_far = level_swaps(branch_parts)
    hidden, grads_middle = ordered(hidden, grads_middle)
    grad_down = outer_one(hidden[0], seen_cot, down_groups)
    grads_last, grad_down = ordered(grads_last, grad_down)

    grads, normed_mine, normed_theirs = contract(
        [grads_share, grads_x, grads_y, *grads_last], [gate_weight, up_weight], [gate_mask, up_mask], last_plan, (F32, BF16), False
    )
    branch_far, normed_mine, normed_theirs = ordered(branch_far, normed_mine, normed_theirs)

    kept, *parts, down_sum = owner(place_arg, normed_mine, core_swap(normed_theirs), cols, normed_own)
    grads, parts, down_sum, inner = ordered(grads, parts, down_sum, inner)
    far = level_swaps(parts)
    down_pair = down_sum + swap(down_sum, "col", cols, 1)
    inner_pair = inner + row_swap(inner, 1)
    grads, down_pair, inner_pair = ordered(grads, down_pair, inner_pair)
    down_got = swap(down_pair, "col", cols, 2)
    inner_got = row_swap(inner_pair, 2)
    grad_gate, grad_up = outer(seen_rows, grads, [gate_groups, up_groups])
    far, down_got, inner_got, grad_gate, grad_up = ordered(far, down_got, inner_got, grad_gate, grad_up)
    inner = inner_pair + inner_got
    down_levels = down_pair + down_got
    down_total = down_levels + core_swap(down_levels)
    branch = owner_total(branch_kept, branch_far).astype(BF16)
    normed_grad = owner_total(kept, far)
    grad_gain = down_total.reshape(features) / norm_gain
    grad_tokens = (
        inv_rms * norm_gain * normed_grad - token_f * inv_rms * inv_rms * inner[:, :1] / (features * rows)
    )
    return (branch, grad_tokens, grad_gain, grad_gate, grad_up, grad_down)


def general_device(
    tokens, norm_gain, gate_weight, up_weight, down_weight, gate_keep, up_keep, down_keep, cotangent
):
    owners = ("dp", "col")
    features = tokens.shape[1]
    place_arg = jnp.zeros((1,), jnp.int32)
    token_f = tokens.astype(F32)
    square = lax.psum(jnp.sum(token_f * token_f, axis=1), "row")
    inv_rms = lax.rsqrt(square[:, None] / (features * lax.axis_size("row")) + 1e-05)
    normed = (token_f * inv_rms * norm_gain).astype(BF16)
    gate_mask, up_mask, down_mask = widen(gate_keep), widen(up_keep), widen(down_keep)
    gate_groups, up_groups, down_groups = widen_grouped(gate_keep), widen_grouped(up_keep), widen_grouped(down_keep)
    seen_cot = lax.all_gather(cotangent, owners, axis=0, tiled=True)
    seen_rows = lax.all_gather(normed, owners, axis=0, tiled=True)
    plan = [[(0, seen_cot.shape[0])]]

    def share(value):
        return lax.psum_scatter(value.astype(F32), "row", scatter_dimension=1, tiled=True)

    def collect(value):
        return lax.all_gather(value.astype(BF16), "row", axis=1, tiled=True)

    def owner_sum(value):
        return lax.psum_scatter(value, owners, scatter_dimension=0, tiled=True)

    _, one = project(place_arg, [seen_cot], [down_weight], [down_mask], plan, True)
    _, pair = project(place_arg, [seen_rows], [gate_weight, up_weight], [gate_mask, up_mask], plan, False)
    pair = share(pair)
    hidden, gate_grad, up_grad = activation(pair[0], pair[1], share(one)[0])
    hidden, branch = contract([collect(hidden[None])], [down_weight], [down_mask], plan, (F32,), True)
    branch = owner_sum(branch).astype(BF16)
    grads, normed_grad = contract(
        [collect(jnp.stack([gate_grad, up_grad]))], [gate_weight, up_weight], [gate_mask, up_mask], plan, (F32,), False
    )
    normed_grad = owner_sum(normed_grad)
    grad_down = outer_one(hidden[0], seen_cot, down_groups)
    grad_gate, grad_up = outer(seen_rows, grads, [gate_groups, up_groups])
    grad_tokens, grad_gain = finish(
        token_f,
        inv_rms,
        norm_gain,
        normed_grad,
        lambda value: lax.psum(value, "row"),
        lambda value: lax.psum(value, owners),
    )
    return (branch, grad_tokens, grad_gain, grad_gate, grad_up, grad_down)


def solution(mesh):
    split = P(("dp", "col"), "row")
    turned = P("row", ("dp", "col"))
    sizes = (mesh.shape["dp"], mesh.shape["row"], mesh.shape["col"])
    on_device = exchange_device if sizes == (2, 4, 4) else general_device
    return jax.shard_map(
        on_device,
        mesh=mesh,
        in_specs=(split, P("row"), turned, turned, split, turned, turned, split, split),
        out_specs=(split, split, P("row"), turned, turned, split),
        check_vma=False,
    )
```
